128 devices in a mesh: seq: 16 (over x_hi, z, core), blk: 8 (over y, x_lo).
Axes of the slice: x: 4 (x_hi: 2, x_lo: 2; x = x_hi * 2 + x_lo), y: 4, z: 4, core: 2. Of those that a mesh axis runs over, the one named last changes fastest.
Arguments:
- tokens: bfloat16 [16384, 3072], P(('seq', 'blk')), may hold values from -8.6 to 8.6
- project_weight: bfloat16 [3, 3072, 2048], P(None, None, 'seq')
- noisy_latent: float32 [16384, 64], P(('seq', 'blk')), may hold values from -6 to 6
- final_weight: bfloat16 [2048, 64], replicated, may hold values from -0.5 to 0.5
- conv_weight: bfloat16 [432, 512], replicated, may hold values from -0.3125 to 0.3125
- norm_gain: float32 [512], replicated, may hold values from 0.1 to 1.9
- norm_shift: float32 [512], replicated, may hold values from -3 to 3
- owner_count: int32 [128], replicated, may hold values from 1 to 4, 256 in all
- intersection: int32 [256, 4], replicated, may hold values from 0 to 127, as said below
Outputs:
- decoded: bfloat16 [128, 4, 512, 2048], P(('seq', 'blk'))
The draws below stay inside these ranges and needn't reach their ends.
Inputs may be any that keep to these rules, and one draw needn't show every extreme that they name: Owner o holds pixel tiles s to s + owner_count[o] - 1, s the sum of the counts below o; the counts sum to 256 and one owner holds exactly 4. `intersection`: row p names the four latent tiles of a 2 x 2 block of neighbouring tiles on a grid of 16 rows by 8 columns, tile r * 8 + c at row r, column c, in the order top left, top right, bottom left, bottom right.
All inputs are finite; a program needn't handle non-finite values.
Results may differ from the reference program's by a relative error of at most 0.014.
Values may be sent and summed in bfloat16 or wider, within the bound.
No kernel may reach another device: no remote copies, remote signals or barrier semaphores. Data moves between devices by JAX's collectives and lax.ppermute only.
A program may use at most 128 MiB of HBM per device.

```python
import math
import jax
import jax.numpy as jnp
import numpy as np
from jax import lax

D = 3072
HEAD_DIM = 128
HEADS = 16
LATENT_CH = 16
CH = 512
GROUPS = 32
TILE_F = 2
TILE_PH = 8
TILE_PW = 8
MAXPIX = 4
TOKENS = 16384
PATCH_CH = 64
PIXEL_TILES = 256
TILE_ROWS = 16
TILE_COLS = 8
DEVICES = 128


def draw_tokens(key, part):
    key = jax.random.fold_in(key, 11)
    base_key = jax.random.fold_in(key, 0)
    return jnp.clip(jax.random.normal(base_key, (TOKENS, D), jnp.float32), -6.0, 6.0).astype(jnp.bfloat16)


def draw_project_weight(key, part):
    key = jax.random.fold_in(key, 23)
    first_key, second_key, third_key = jax.random.split(key, 3)
    matrix_shape = (D, HEADS * HEAD_DIM)
    spread = D ** (-0.5)
    query_part = jnp.clip(jax.random.normal(first_key, matrix_shape, jnp.float32), -6.0, 6.0) * (2.0 * spread)
    key_part = jnp.clip(jax.random.normal(second_key, matrix_shape, jnp.float32), -6.0, 6.0) * (2.0 * spread)
    value_part = jnp.clip(jax.random.normal(third_key, matrix_shape, jnp.float32), -6.0, 6.0) * spread
    return jnp.stack([query_part, key_part, value_part]).astype(jnp.bfloat16)


def draw_intersection(key, part):
    key = jax.random.fold_in(key, 37)
    row_key, column_key = jax.random.split(key)
    anchor_row = jax.random.randint(row_key, (PIXEL_TILES,), 0, TILE_ROWS - 1)
    anchor_col = jax.random.randint(column_key, (PIXEL_TILES,), 0, TILE_COLS - 1)
    anchor_row = anchor_row.at[0].set(0).at[PIXEL_TILES - 1].set(TILE_ROWS - 2)
    anchor_col = anchor_col.at[0].set(0).at[PIXEL_TILES - 1].set(TILE_COLS - 2)
    corner = anchor_row * TILE_COLS + anchor_col
    return jnp.stack([corner, corner + 1, corner + TILE_COLS, corner + TILE_COLS + 1], axis=1).astype(jnp.int32)


def shard_levels(stream_key, shape, shards, low, top_value):
    def one(position, parts):
        heights = jax.random.uniform(jax.random.fold_in(jax.random.fold_in(stream_key, 6), position), (parts,), jnp.float32, low / len(shards), top_value / len(shards))
        return jnp.repeat(jnp.exp(heights), shape[position] // parts).reshape((-1,) + (1,) * (len(shape) - position - 1))

    loudness = one(*shards[0])
    for cut in shards[1:]:
        loudness = loudness * one(*cut)
    return loudness


def length_profile(number_of, total, most, lean):
    portions = [(1 << 20) // math.isqrt(rank ** lean) + 1 for rank in range(2, number_of + 1)]
    rest, holding = total - most - (number_of - 1), [1] * (number_of - 1)
    while rest > 0:
        movable = [i for i in range(number_of - 1) if holding[i] < most]
        pool, remaining = sum([portions[i] for i in movable]), rest
        for i in movable:
            more = min(most - holding[i], max(1, remaining * portions[i] // pool), rest)
            holding[i] = holding[i] + more
            rest = rest - more
    return np.array([most] + holding)


def uneven(own_key, amount, total, bound, skew):
    if amount == 2:
        one = jax.random.randint(own_key, (), max(1, total - bound), min(bound, total - 1) + 1)
        return jnp.stack([one, total - one])
    tallies = jnp.asarray(length_profile(amount, total, bound, skew), jnp.int32)
    twos = (amount - 1) // 2
    donor, taker = tallies[1:1 + 2 * twos:2], tallies[2:2 + 2 * twos:2]
    margin = jnp.minimum(donor - 1, bound - taker)
    moved = jax.random.randint(jax.random.fold_in(own_key, 1), (twos,), 0, 1 << 20) % (margin + 1)
    tallies = tallies.at[1:1 + 2 * twos:2].set(donor - moved).at[2:2 + 2 * twos:2].set(taker + moved)
    return tallies[jax.random.permutation(jax.random.fold_in(own_key, 2), amount)]


def gaussian(own_key, dims, scale, limit, cuts=(), held_as=jnp.bfloat16):
    level = shard_levels(own_key, dims, cuts, -0.22, 0.18) if cuts else 1.0
    array = jax.random.normal(own_key, dims, jnp.float32) * scale * level
    return jnp.minimum(jnp.maximum(array, -limit), limit).astype(held_as)


def setup_inputs(seed: int = 0) -> dict:
    key_list = jax.random.split(jax.random.key(seed), 10)
    return {
        "tokens": draw_tokens(jax.random.fold_in(key_list[9], 71), 0),
        "project_weight": draw_project_weight(jax.random.fold_in(key_list[9], 71), 0),
        "noisy_latent": gaussian(key_list[2], (TOKENS, PATCH_CH), 1.0, 6.0, ((0, 128),), jnp.float32),
        "final_weight": gaussian(key_list[3], (HEADS * HEAD_DIM, PATCH_CH), (HEADS * HEAD_DIM // 16) ** -0.5, 0.5),
        "conv_weight": gaussian(key_list[4], (27 * LATENT_CH, CH), (27 * LATENT_CH) ** -0.5, 0.3125),
        "norm_gain": jnp.clip(1.0 + 0.18 * jax.random.normal(key_list[5], (CH,), jnp.float32), 0.1, 1.9),
        "norm_shift": gaussian(key_list[6], (CH,), 0.5, 3.0, (), jnp.float32),
        "owner_count": uneven(key_list[7], DEVICES, PIXEL_TILES, MAXPIX, 2).astype(jnp.int32),
        "intersection": draw_intersection(jax.random.fold_in(key_list[9], 71), 0),
    }


scale_factor = 0.476986
step_size = 0.25
norm_eps = 1e-06

def decode_tile(all_tiles, tile_ids, conv_weight, norm_gain, norm_shift):
    pieces = all_tiles[tile_ids]
    upper = jnp.concatenate([pieces[0], pieces[1]], axis=3)
    lower = jnp.concatenate([pieces[2], pieces[3]], axis=3)
    region = jnp.concatenate([upper, lower], axis=2)
    padded = jnp.pad(region, ((0, 0), (2, 0), (1, 1), (1, 1)), mode='edge')
    frames = region.shape[1]
    height = region.shape[2]
    breadth = region.shape[3]
    tap_list = []
    for tap_time in range(3):
        for tap_row in range(3):
            for tap_col in range(3):
                window = padded[:, tap_time:tap_time + frames, tap_row:tap_row + height, tap_col:tap_col + breadth]
                tap_list.append(window.reshape(region.shape[0], -1))
    patches = jnp.concatenate(tap_list, axis=0)
    convolved = lax.dot_general(conv_weight, patches, (((0,), (0,)), ((), ())), preferred_element_type=jnp.float32)
    channels = convolved.shape[0]
    grouped = convolved.reshape(GROUPS, channels // GROUPS, -1)
    group_mean = lax.optimization_barrier(jnp.mean(grouped, axis=(1, 2), keepdims=True))
    group_var = lax.optimization_barrier(jnp.mean(jnp.square(grouped - group_mean), axis=(1, 2), keepdims=True))
    normed = ((grouped - group_mean) * lax.rsqrt(group_var + norm_eps)).reshape(channels, -1)
    normed = normed * norm_gain[:, None] + norm_shift[:, None]
    return jax.nn.silu(normed).astype(jnp.bfloat16)

def attend_head(head_data):
    queries, key_rows, value_rows = head_data
    query_block = min(2048, queries.shape[0])
    blocks = queries.reshape(-1, query_block, queries.shape[1])
    inv_root = queries.shape[1] ** (-0.5)

    def one_block(query_rows):
        scores = jnp.dot(query_rows, key_rows.T, preferred_element_type=jnp.float32) * inv_root
        row_max = lax.optimization_barrier(jnp.max(scores, axis=1, keepdims=True))
        exp_scores = jnp.exp(scores - row_max)
        denominator = lax.optimization_barrier(jnp.sum(exp_scores, axis=1, keepdims=True))
        numerator = jnp.dot(exp_scores.astype(jnp.bfloat16), value_rows, preferred_element_type=jnp.float32)
        return (numerator / denominator).astype(jnp.bfloat16)
    return lax.map(one_block, blocks).reshape(queries.shape)

def reference(tokens, project_weight, noisy_latent, final_weight, conv_weight, norm_gain, norm_shift, owner_count, intersection):
    projected = []
    for proj_index in range(3):
        product = jnp.dot(tokens, project_weight[proj_index], preferred_element_type=jnp.float32).astype(jnp.bfloat16)
        projected.append(product.reshape(TOKENS, HEADS, HEAD_DIM).transpose(1, 0, 2))
    attended = lax.map(attend_head, (projected[0], projected[1], projected[2]))
    attended = attended.transpose(1, 0, 2).reshape(TOKENS, HEADS * HEAD_DIM)
    velocity = jnp.dot(attended, final_weight, preferred_element_type=jnp.float32)
    latent = (noisy_latent - step_size * velocity) / scale_factor
    tiles = latent.reshape(DEVICES, TILE_F, TILE_PH, TILE_PW, LATENT_CH, 2, 2).transpose(0, 4, 1, 2, 5, 3, 6)
    tiles = tiles.reshape(DEVICES, LATENT_CH, TILE_F, 2 * TILE_PH, 2 * TILE_PW).astype(jnp.bfloat16)
    pixel = lax.map(lambda tile_ids: decode_tile(tiles, tile_ids, conv_weight, norm_gain, norm_shift), intersection)
    count_ends = jnp.cumsum(owner_count, dtype=jnp.int32)
    first_tile = count_ends - owner_count
    slot_range = jnp.arange(MAXPIX, dtype=jnp.int32)
    slot_tiles = jnp.minimum(first_tile[:, None] + slot_range[None, :], PIXEL_TILES - 1).astype(jnp.int32)
    occupied = slot_range[None, :] < owner_count[:, None]
    picked = pixel[slot_tiles]
    return jnp.where(occupied[:, :, None, None], picked, jnp.zeros((), jnp.bfloat16))
```

```python
import functools

import jax
import jax.numpy as jnp
import numpy as np
from jax import lax
from jax.experimental import pallas as pl
from jax.experimental.pallas import tpu as pltpu
from jax.sharding import Mesh
from jax.sharding import PartitionSpec as P

HEAD_DIM = 128
LATENT_CH = 16
PATCH = 4
GROUPS = 32
MAXPIX = 4

scale_factor = 0.476986
step_size = 0.25
norm_eps = 1e-06

AXES = ("xh", "z", "c", "y", "xl")
SIZES = (2, 4, 2, 4, 2)
SEQ = ("xh", "z", "c")

NT = (((1,), (1,)), ((), ()))
LOG2E = 1.4426950408889634
PAYLOAD = 80


def shift(x, **moves):
    pairs = []
    for source in range(int(np.prod(SIZES))):
        place = np.unravel_index(source, SIZES)
        target = [(p + moves.get(a, 0)) % n for p, a, n in zip(place, AXES, SIZES)]
        pairs.append((source, int(np.ravel_multi_index(target, SIZES))))
    return lax.ppermute(x, AXES, pairs)


def attention_kernel(bk, nk, xl_ref, q_ref, k_ref, v_ref, w_ref, out_ref, ve_ref):
    @pl.when((pl.program_id(0) == 0) & (pl.program_id(1) == 0))
    def _():
        ve_ref[:, :HEAD_DIM] = v_ref[...]
        ve_ref[:, HEAD_DIM:] = jnp.ones(v_ref.shape, jnp.bfloat16)

    q = q_ref[0]
    bq = q.shape[0]

    def scores_of(i):
        return lax.dot_general(
            q, k_ref[i * bk : (i + 1) * bk, :], NT, preferred_element_type=jnp.float32
        )

    run_max = jnp.full((bq, 1), -1e30, jnp.float32)
    acc = None
    following = scores_of(0)
    for i in range(nk):
        scores = following
        if i + 1 < nk:
            following = scores_of(i + 1)
        new_max = jnp.maximum(run_max, jnp.max(scores, axis=1, keepdims=True))
        probs = jnp.exp2(scores - new_max).astype(jnp.bfloat16)
        part = jnp.dot(probs, ve_ref[i * bk : (i + 1) * bk, :], preferred_element_type=jnp.float32)
        acc = part if acc is None else acc * jnp.exp2(run_max - new_max) + part
        run_max = new_max

    total = acc[:, HEAD_DIM:]
    attended = (acc[:, :HEAD_DIM] / total).astype(jnp.bfloat16)
    velocity = lax.dot_general(w_ref[...], attended, NT, preferred_element_type=jnp.float32)
    log_sum = run_max + jnp.log2(total)
    high = log_sum.astype(jnp.bfloat16)
    rest = log_sum - high.astype(jnp.float32)
    mid = rest.astype(jnp.bfloat16)
    low = (rest - mid.astype(jnp.float32)).astype(jnp.bfloat16)
    lane = lax.broadcasted_iota(jnp.int32, (bq, HEAD_DIM), 1)
    terms = jnp.where(
        lane == 0,
        high.astype(jnp.float32),
        jnp.where(lane == 1, mid.astype(jnp.float32), low.astype(jnp.float32)),
    ).astype(jnp.bfloat16)
    row = lax.broadcasted_iota(jnp.int32, (16, HEAD_DIM), 0)
    column = lax.broadcasted_iota(jnp.int32, (16, HEAD_DIM), 1)
    pick = ((row == column) & (row < 3)).astype(jnp.float32).astype(jnp.bfloat16)
    stats = lax.dot_general(pick, terms, NT, preferred_element_type=jnp.float32)
    joined = jnp.concatenate([velocity, stats], axis=0).astype(jnp.bfloat16)
    for t in range(bq // 128):
        out_ref[t, 0] = joined[:, t * 128 : (t + 1) * 128]


def attention(q, kv, w, my_xl, bq=1024, bk=512):
    rows = q.shape[1]
    length = kv.shape[0]
    blocks = rows // 128
    return pl.pallas_call(
        functools.partial(attention_kernel, bk, length // bk),
        grid_spec=pltpu.PrefetchScalarGridSpec(
            num_scalar_prefetch=1,
            grid=(2, rows // bq),
            in_specs=[
                pl.BlockSpec((1, bq, HEAD_DIM), lambda o, i, xl: (o, i, 0)),
                pl.BlockSpec((length, HEAD_DIM), lambda o, i, xl: (0, 0)),
                pl.BlockSpec((length, HEAD_DIM), lambda o, i, xl: (0, 1)),
                pl.BlockSpec((64, HEAD_DIM), lambda o, i, xl: (0, 0)),
            ],
            out_specs=pl.BlockSpec(
                (bq // 128, 1, PAYLOAD, 128), lambda o, i, xl: (i, (xl[0] + o) % 2, 0, 0)
            ),
            scratch_shapes=[pltpu.VMEM((length, 2 * HEAD_DIM), jnp.bfloat16)],
        ),
        out_shape=jax.ShapeDtypeStruct((blocks, 2, PAYLOAD, 128), jnp.bfloat16),
        compiler_params=pltpu.CompilerParams(vmem_limit_bytes=56 << 20),
        name="attention",
    )(my_xl, q, kv, kv, w)


def combine_kernel(parts_ref, noisy_ref, out_ref):
    velocity = jnp.zeros((64, 128), jnp.float32)
    for head in range(parts_ref.shape[0] // 2):
        logs = []
        for half in range(2):
            terms = parts_ref[2 * head + half, 64:PAYLOAD, :].astype(jnp.float32)
            logs.append(terms[0:1] + terms[1:2] + terms[2:3])
        top = jnp.maximum(logs[0], logs[1])
        first, second = jnp.exp2(logs[0] - top), jnp.exp2(logs[1] - top)
        inverse = 1.0 / (first + second)
        velocity += parts_ref[2 * head, 0:64, :].astype(jnp.float32) * (first * inverse)
        velocity += parts_ref[2 * head + 1, 0:64, :].astype(jnp.float32) * (second * inverse)
    latent = (noisy_ref[...] - step_size * velocity) / scale_factor
    out_ref[...] = latent.astype(jnp.bfloat16)


def combine(parts, noisy):
    return pl.pallas_call(
        combine_kernel,
        out_shape=jax.ShapeDtypeStruct((64, 128), jnp.bfloat16),
        name="latent_tile",
    )(parts, noisy)


def placing_matrix():
    side, p, q, f, i, j = np.meshgrid(*[np.arange(n) for n in (2, 2, 2, 2, 8, 8)], indexing="ij")
    target = f * 512 + (2 * i + p) * 32 + side * 16 + 2 * j + q
    place = np.zeros((1024, 1024), np.float32)
    place[np.arange(1024), target.reshape(-1)] = 1.0
    return place


def decode_kernel(
    ids_ref, tiles_ref, place_ref, first_ref, second_ref, gain_ref, shift_ref, out_ref, wide_ref, half_ref, patch_ref, conv_ref
):
    slot = pl.program_id(0)

    @pl.when(slot == 0)
    def _():
        for s in range(MAXPIX):
            for half in range(2):
                for side in range(2):
                    tile = tiles_ref[ids_ref[1 + s * 4 + half * 2 + side]]
                    for pq in range(4):
                        column = (side * 4 + pq) * 128
                        row = (s * 2 + half) * 16
                        wide_ref[row : row + 16, column : column + 128] = tile[pq * 16 : pq * 16 + 16, :]
        half_ref[...] = jnp.dot(wide_ref[...], place_ref[...], preferred_element_type=jnp.float32)

    @pl.when(slot >= ids_ref[0])
    def _():
        out_ref[...] = jnp.zeros(out_ref.shape, out_ref.dtype)

    @pl.when(slot < ids_ref[0])
    def _():
        start = pl.multiple_of(slot * 32, 32)
        both = half_ref[pl.ds(start, 32), :]
        frames = []
        for f in range(2):
            frames.append(
                jnp.concatenate(
                    [both[0:16, f * 512 : f * 512 + 512], both[16:32, f * 512 : f * 512 + 512]], axis=1
                )
            )
        region = jnp.concatenate(frames, axis=0)
        lane = lax.broadcasted_iota(jnp.int32, region.shape, 1)
        column = lane % 32
        for g in range(3):
            if g == 0:
                across = jnp.where(column == 0, region, pltpu.roll(region, 1, 1))
            elif g == 1:
                across = region
            else:
                across = jnp.where(column == 31, region, pltpu.roll(region, 1023, 1))
            for b in range(3):
                if b == 0:
                    tap = jnp.where(lane < 32, across, pltpu.roll(across, 32, 1))
                elif b == 1:
                    tap = across
                else:
                    tap = jnp.where(lane >= 992, across, pltpu.roll(across, 992, 1))
                row = (b * 3 + g) * 16
                tap = tap.astype(jnp.bfloat16)
                patch_ref[row : row + 16, :] = tap[0:16]
                patch_ref[144 + row : 144 + row + 16, :] = tap[16:32]
        conv_ref[:, :1024] = jnp.dot(
            first_ref[...], patch_ref[0:144, :], preferred_element_type=jnp.float32
        )
        conv_ref[:, 1024:] = jnp.dot(
            second_ref[...], patch_ref[...], preferred_element_type=jnp.float32
        )
        size = conv_ref.shape[0] // GROUPS
        count = 1.0 / (size * conv_ref.shape[1])
        for group in range(GROUPS):
            rows = slice(group * size, (group + 1) * size)
            values = conv_ref[rows, :]
            mean = jnp.sum(jnp.sum(values, axis=0, keepdims=True), axis=1, keepdims=True) * count
            apart = values - mean
            squares = apart * apart
            var = jnp.sum(jnp.sum(squares, axis=0, keepdims=True), axis=1, keepdims=True) * count
            scale = gain_ref[rows, :] * lax.rsqrt(var + norm_eps) * 0.5
            half_norm = apart * scale + shift_ref[rows, :] * 0.5
            out_ref[0, 0, rows, :] = (half_norm + half_norm * jnp.tanh(half_norm)).astype(jnp.bfloat16)


def decode(ids, tiles, place, first, second, gain, shift_rows):
    channels = first.shape[0]
    whole = lambda shape: pl.BlockSpec(shape, lambda s, ids: (0,) * len(shape))
    return pl.pallas_call(
        decode_kernel,
        grid_spec=pltpu.PrefetchScalarGridSpec(
            num_scalar_prefetch=1,
            grid=(MAXPIX,),
            in_specs=[
                whole(tiles.shape),
                whole(place.shape),
                whole(first.shape),
                whole(second.shape),
                whole(gain.shape),
                whole(shift_rows.shape),
            ],
            out_specs=pl.BlockSpec((1, 1, channels, 2048), lambda s, ids: (0, s, 0, 0)),
            scratch_shapes=[
                pltpu.VMEM((128, 1024), jnp.bfloat16),
                pltpu.VMEM((128, 1024), jnp.float32),
                pltpu.VMEM((288, 1024), jnp.bfloat16),
                pltpu.VMEM((channels, 2048), jnp.float32),
            ],
        ),
        out_shape=jax.ShapeDtypeStruct((1, MAXPIX, channels, 2048), jnp.bfloat16),
        compiler_params=pltpu.CompilerParams(vmem_limit_bytes=56 << 20),
        name="decode",
    )(ids, tiles, place, first, second, gain, shift_rows)


def body(
    tokens,
    project_weight,
    noisy_latent,
    final_weight,
    conv_weight,
    norm_gain,
    norm_shift,
    owner_count,
    intersection,
):
    my_xl = lax.axis_index("xl")
    head = lax.axis_index(SEQ)

    gathered = lax.all_gather(tokens, SEQ, axis=0, tiled=True)
    own_q = jnp.dot(gathered, project_weight[0], preferred_element_type=jnp.float32)
    own_q = (own_q * (LOG2E * HEAD_DIM**-0.5)).astype(jnp.bfloat16)
    own_kv = jnp.dot(
        gathered,
        jnp.concatenate([project_weight[1], project_weight[2]], axis=1),
        preferred_element_type=jnp.float32,
    ).astype(jnp.bfloat16)
    queries = jnp.stack([own_q, shift(own_q, xl=1)])
    kv = lax.all_gather(own_kv, "y", axis=0, tiled=True)

    w = lax.dynamic_slice_in_dim(final_weight, head * HEAD_DIM, HEAD_DIM, axis=0)
    w = w.reshape(HEAD_DIM, LATENT_CH, PATCH).transpose(2, 1, 0).reshape(64, HEAD_DIM)
    noisy = noisy_latent.reshape(-1, LATENT_CH, PATCH).transpose(2, 1, 0).reshape(64, -1)

    parts = attention(queries, kv, w, my_xl.astype(jnp.int32).reshape(1))
    parts = parts.reshape(-1, PAYLOAD, 128)
    parts = lax.all_to_all(parts, SEQ + ("xl",), split_axis=0, concat_axis=0, tiled=True)
    tile = combine(parts, noisy)

    tiles = lax.all_to_all(
        jnp.broadcast_to(tile[None], (128,) + tile.shape), AXES, split_axis=0, concat_axis=0, tiled=True
    )

    rank = lax.axis_index(AXES)
    ends = jnp.cumsum(owner_count, dtype=jnp.int32)
    count = owner_count[rank]
    slots = jnp.minimum(ends[rank] - count + jnp.arange(MAXPIX), intersection.shape[0] - 1)
    ids = jnp.concatenate([count[None], intersection[slots].reshape(-1)]).astype(jnp.int32)

    taps = conv_weight.astype(jnp.float32).reshape(3, -1, conv_weight.shape[1])
    first = (taps[0] + taps[1] + taps[2]).T.astype(jnp.bfloat16)
    second = jnp.concatenate([taps[0] + taps[1], taps[2]], axis=0).T.astype(jnp.bfloat16)
    place = jnp.asarray(placing_matrix(), jnp.bfloat16)
    return decode(ids, tiles, place, first, second, norm_gain[:, None], norm_shift[:, None])


def solution(mesh):
    fine = Mesh(mesh.devices.reshape(SIZES), AXES)
    blk = ("y", "xl")
    return jax.shard_map(
        body,
        mesh=fine,
        in_specs=(
            P(SEQ + blk, None),
            P(None, None, SEQ),
            P(SEQ + blk, None),
            P(),
            P(),
            P(),
            P(),
            P(),
            P(),
        ),
        out_specs=P(SEQ + blk, None, None, None),
        check_vma=False,
    )
```

```python
import functools

import jax
import jax.numpy as jnp
import numpy as np
from jax import lax
from jax.experimental import pallas as pl
from jax.experimental.pallas import tpu as pltpu
from jax.sharding import Mesh
from jax.sharding import PartitionSpec as P

HEAD_DIM = 128
LATENT_CH = 16
PATCH = 4
GROUPS = 32
MAXPIX = 4

scale_factor = 0.476986
step_size = 0.25
norm_eps = 1e-06

AXES = ("xh", "z", "c", "y", "xl")
SIZES = (2, 4, 2, 4, 2)
SEQ = ("xh", "z", "c")

NT = (((1,), (1,)), ((), ()))
LOG2E = 1.4426950408889634
PAYLOAD = 80


def shift(x, **moves):
    pairs = []
    for source in range(int(np.prod(SIZES))):
        place = np.unravel_index(source, SIZES)
        target = [(p + moves.get(a, 0)) % n for p, a, n in zip(place, AXES, SIZES)]
        pairs.append((source, int(np.ravel_multi_index(target, SIZES))))
    return lax.ppermute(x, AXES, pairs)


def project_kernel(steps, scale, n_after, *refs):
    x_refs, refs = refs[: len(steps)], refs[len(steps) :]
    w_ref, out_refs = refs[0], refs[1 + n_after :]
    step = pl.program_id(0)
    start = 0
    for x_ref, count in zip(x_refs, steps):

        def multiply(x_ref=x_ref):
            out = jnp.dot(x_ref[...], w_ref[...], preferred_element_type=jnp.float32)
            column = 0
            for n, out_ref in enumerate(out_refs):
                width = out_ref.shape[1]
                part = out[:, column : column + width]
                out_ref[...] = (part * scale if n % 2 == 0 else part).astype(jnp.bfloat16)
                column += width

        pl.when((step >= start) & (step < start + count))(multiply)
        start += count


def project(xs, w, scale, after=(), bm=256):
    steps = [x.shape[0] // bm for x in xs]
    starts = np.cumsum([0] + steps)
    rows = int(starts[-1]) * bm
    widths = [HEAD_DIM, 2 * HEAD_DIM] * 2
    in_specs = [
        pl.BlockSpec((bm, x.shape[1]), lambda i, a=int(a), n=n: (jnp.clip(i - a, 0, n - 1), 0))
        for x, a, n in zip(xs, starts, steps)
    ]
    in_specs.append(pl.BlockSpec(w.shape, lambda i: (0, 0)))
    in_specs += [pl.BlockSpec(memory_space=pl.ANY)] * len(after)
    return pl.pallas_call(
        functools.partial(project_kernel, steps, scale, len(after)),
        grid=(rows // bm,),
        in_specs=in_specs,
        out_specs=[pl.BlockSpec((bm, width), lambda i: (i, 0)) for width in widths],
        out_shape=[jax.ShapeDtypeStruct((rows, width), jnp.bfloat16) for width in widths],
        compiler_params=pltpu.CompilerParams(vmem_limit_bytes=56 << 20),
        name="project",
    )(*xs, w, *after)


def softmax_blocks(q, kv_refs, value_ref, bk, run_max, acc):
    places, start = [], 0
    for ref in kv_refs:
        for i in range(0, ref.shape[0], bk):
            places.append((ref, i, start + i))
        start += ref.shape[0]

    def scores_of(n):
        ref, i, _ = places[n]
        return lax.dot_general(
            q, ref[i : i + bk, :HEAD_DIM], NT, preferred_element_type=jnp.float32
        )

    following = scores_of(0)
    for n, (_, _, row) in enumerate(places):
        scores = following
        if n + 1 < len(places):
            following = scores_of(n + 1)
        new_max = jnp.max(scores, axis=1, keepdims=True)
        if run_max is not None:
            new_max = jnp.maximum(run_max, new_max)
        probs = jnp.exp2(scores - new_max).astype(jnp.bfloat16)
        part = jnp.dot(probs, value_ref[row : row + bk, :], preferred_element_type=jnp.float32)
        acc = part if acc is None else acc * jnp.exp2(run_max - new_max) + part
        run_max = new_max
    return run_max, acc


def attention_kernel(bk, n_kv, carry_in, n_into, final, *refs):
    if final:
        place_ref, *refs = refs
    q_ref, *refs = refs
    kv_refs, refs = refs[:n_kv], refs[n_kv:]
    if carry_in:
        acc_in_ref, max_in_ref, *refs = refs
    refs = refs[n_into:]
    if final:
        w_ref, out_ref, value_ref = refs
    else:
        acc_out_ref, max_out_ref, value_ref = refs

    @pl.when(pl.program_id(0) == 0)
    def _():
        start = 0
        for ref in kv_refs:
            n = ref.shape[0]
            value_ref[start : start + n, :HEAD_DIM] = ref[:, HEAD_DIM:]
            value_ref[start : start + n, HEAD_DIM:] = jnp.ones((n, HEAD_DIM), jnp.bfloat16)
            start += n

    q = q_ref[...]
    bq = q.shape[0]
    run_max, acc = None, None
    if carry_in:
        run_max, acc = jnp.max(max_in_ref[...], axis=1, keepdims=True), acc_in_ref[...]
    run_max, acc = softmax_blocks(q, kv_refs, value_ref, bk, run_max, acc)
    if not final:
        acc_out_ref[...] = acc
        max_out_ref[...] = jnp.broadcast_to(run_max, max_out_ref.shape)
        return

    total = acc[:, HEAD_DIM:]
    attended = (acc[:, :HEAD_DIM] / total).astype(jnp.bfloat16)
    velocity = lax.dot_general(w_ref[...], attended, NT, preferred_element_type=jnp.float32)
    log_sum = run_max + jnp.log2(total)
    high = log_sum.astype(jnp.bfloat16).astype(jnp.float32)
    mid = (log_sum - high).astype(jnp.bfloat16).astype(jnp.float32)
    low = log_sum - high - mid
    lane = lax.broadcasted_iota(jnp.int32, (bq, HEAD_DIM), 1)
    terms = jnp.where(lane == 0, high, jnp.where(lane == 1, mid, low)).astype(jnp.bfloat16)
    row = lax.broadcasted_iota(jnp.int32, (PAYLOAD - 64, HEAD_DIM), 0)
    column = lax.broadcasted_iota(jnp.int32, (PAYLOAD - 64, HEAD_DIM), 1)
    pick = ((row == column) & (row < 3)).astype(jnp.float32).astype(jnp.bfloat16)
    stats = lax.dot_general(pick, terms, NT, preferred_element_type=jnp.float32)
    joined = jnp.concatenate([velocity, stats], axis=0).astype(jnp.bfloat16)
    cores, depth = out_ref.shape[2], out_ref.shape[1]
    for core in range(cores):
        for z in range(depth):
            t = core * depth + z
            out_ref[0, z, (core + place_ref[2]) % cores, 0] = joined[:, t * 128 : (t + 1) * 128]


def attention(q, kvs, carry=None, into=None, rows_out=None, last=None, bq=1024, bk=512):
    rows = q.shape[0]
    rows_out = rows_out or rows
    skip = 0
    length = sum(kv.shape[0] for kv in kvs)
    by_row = lambda width: pl.BlockSpec((bq, width), lambda i, *p: (i, 0))
    whole = lambda x: pl.BlockSpec(x.shape, lambda i, *p: (0, 0))
    operands, in_specs = [q, *kvs], [by_row(HEAD_DIM)] + [whole(kv) for kv in kvs]
    if carry is not None:
        operands += carry
        in_specs += [by_row(2 * HEAD_DIM), by_row(HEAD_DIM)]
    aliases = {}
    if into is not None:
        aliases = {len(operands): 0, len(operands) + 1: 1}
        operands += into
        in_specs += [pl.BlockSpec(memory_space=pl.ANY)] * 2
        rows_out = into[0].shape[0]
        skip = (rows_out - rows) // bq
    if last is None:
        prefetch = []
        out_specs = [
            pl.BlockSpec((bq, width), lambda i: (i + skip, 0)) for width in (2 * HEAD_DIM, HEAD_DIM)
        ]
        out_shape = [
            jax.ShapeDtypeStruct((rows_out, 2 * HEAD_DIM), jnp.float32),
            jax.ShapeDtypeStruct((rows_out, HEAD_DIM), jnp.float32),
        ]
    else:
        prefetch = [last[0]]
        operands.append(last[1])
        in_specs.append(whole(last[1]))
        out_specs = pl.BlockSpec(
            (1, 4, 2, 1, PAYLOAD, 128),
            lambda i, p: ((i % 2 + p[1]) % 2, 0, 0, (i // 2 + p[0]) % 2, 0, 0),
        )
        out_shape = jax.ShapeDtypeStruct((2, 4, 2, 2, PAYLOAD, 128), jnp.bfloat16)
    return pl.pallas_call(
        functools.partial(
            attention_kernel, bk, len(kvs), carry is not None, len(aliases), last is not None
        ),
        grid_spec=pltpu.PrefetchScalarGridSpec(
            num_scalar_prefetch=len(prefetch),
            grid=(rows // bq,),
            in_specs=in_specs,
            out_specs=out_specs,
            scratch_shapes=[pltpu.VMEM((length, 2 * HEAD_DIM), jnp.bfloat16)],
        ),
        out_shape=out_shape,
        input_output_aliases=aliases,
        compiler_params=pltpu.CompilerParams(vmem_limit_bytes=56 << 20),
        name="attention",
    )(*prefetch, *operands)


def combine_kernel(parts_ref, noisy_ref, out_ref):
    velocity = jnp.zeros((64, 128), jnp.float32)
    for head in range(parts_ref.shape[0] // 2):
        logs = []
        for half in range(2):
            terms = parts_ref[2 * head + half, 64:PAYLOAD, :].astype(jnp.float32)
            logs.append(terms[0:1] + terms[1:2] + terms[2:3])
        top = jnp.maximum(logs[0], logs[1])
        first, second = jnp.exp2(logs[0] - top), jnp.exp2(logs[1] - top)
        inverse = 1.0 / (first + second)
        velocity += parts_ref[2 * head, 0:64, :].astype(jnp.float32) * (first * inverse)
        velocity += parts_ref[2 * head + 1, 0:64, :].astype(jnp.float32) * (second * inverse)
    latent = (noisy_ref[...] - step_size * velocity) / scale_factor
    latent = latent.astype(jnp.bfloat16)
    for n in range(out_ref.shape[0]):
        out_ref[n] = latent


def combine(parts, noisy, copies):
    return pl.pallas_call(
        combine_kernel,
        out_shape=jax.ShapeDtypeStruct((copies, 64, 128), jnp.bfloat16),
        name="latent_tile",
    )(parts, noisy)


def placing_matrix():
    side, p, q, f, i, j = np.meshgrid(*[np.arange(n) for n in (2, 2, 2, 2, 8, 8)], indexing="ij")
    target = f * 512 + (2 * i + p) * 32 + side * 16 + 2 * j + q
    place = np.zeros((1024, 1024), np.float32)
    place[np.arange(1024), target.reshape(-1)] = 1.0
    return place


def decode_kernel(
    ids_ref, own_ref, other_ref, place_ref, first_ref, second_ref, gain_ref, shift_ref, out_ref, wide_ref, half_ref, patch_ref, conv_ref
):
    slot = pl.program_id(0)

    @pl.when(slot == 0)
    def _():
        for s in range(MAXPIX):
            for half in range(2):
                for side in range(2):
                    n = ids_ref[1 + s * 4 + half * 2 + side]
                    tile = jnp.where(n < 64, own_ref[n % 64], other_ref[n % 64])
                    for pq in range(4):
                        column = (side * 4 + pq) * 128
                        row = (s * 2 + half) * 16
                        wide_ref[row : row + 16, column : column + 128] = tile[pq * 16 : pq * 16 + 16, :]
        half_ref[...] = jnp.dot(wide_ref[...], place_ref[...], preferred_element_type=jnp.float32)

    @pl.when(slot >= ids_ref[0])
    def _():
        out_ref[...] = jnp.zeros(out_ref.shape, out_ref.dtype)

    @pl.when(slot < ids_ref[0])
    def _():
        start = pl.multiple_of(slot * 32, 32)
        both = half_ref[pl.ds(start, 32), :]
        frames = []
        for f in range(2):
            frames.append(
                jnp.concatenate(
                    [both[0:16, f * 512 : f * 512 + 512], both[16:32, f * 512 : f * 512 + 512]], axis=1
                )
            )
        region = jnp.concatenate(frames, axis=0)
        lane = lax.broadcasted_iota(jnp.int32, region.shape, 1)
        column = lane % 32
        for g in range(3):
            if g == 0:
                across = jnp.where(column == 0, region, pltpu.roll(region, 1, 1))
            elif g == 1:
                across = region
            else:
                across = jnp.where(column == 31, region, pltpu.roll(region, 1023, 1))
            for b in range(3):
                if b == 0:
                    tap = jnp.where(lane < 32, across, pltpu.roll(across, 32, 1))
                elif b == 1:
                    tap = across
                else:
                    tap = jnp.where(lane >= 992, across, pltpu.roll(across, 992, 1))
                row = (b * 3 + g) * 16
                tap = tap.astype(jnp.bfloat16)
                patch_ref[row : row + 16, :] = tap[0:16]
                patch_ref[144 + row : 144 + row + 16, :] = tap[16:32]
        conv_ref[:, :1024] = jnp.dot(
            first_ref[...], patch_ref[0:144, :], preferred_element_type=jnp.float32
        )
        conv_ref[:, 1024:] = jnp.dot(
            second_ref[...], patch_ref[...], preferred_element_type=jnp.float32
        )
        size = conv_ref.shape[0] // GROUPS
        count = 1.0 / (size * conv_ref.shape[1])
        for group in range(GROUPS):
            rows = slice(group * size, (group + 1) * size)
            values = conv_ref[rows, :]
            mean = jnp.sum(jnp.sum(values, axis=0, keepdims=True), axis=1, keepdims=True) * count
            apart = values - mean
            squares = apart * apart
            var = jnp.sum(jnp.sum(squares, axis=0, keepdims=True), axis=1, keepdims=True) * count
            scale = gain_ref[rows, :] * lax.rsqrt(var + norm_eps) * 0.5
            half_norm = apart * scale + shift_ref[rows, :] * 0.5
            out_ref[0, 0, rows, :] = (half_norm + half_norm * jnp.tanh(half_norm)).astype(jnp.bfloat16)


def decode(ids, own_tiles, other_tiles, place, first, second, gain, shift_rows):
    channels = first.shape[0]
    whole = lambda shape: pl.BlockSpec(shape, lambda s, ids: (0,) * len(shape))
    return pl.pallas_call(
        decode_kernel,
        grid_spec=pltpu.PrefetchScalarGridSpec(
            num_scalar_prefetch=1,
            grid=(MAXPIX,),
            in_specs=[
                whole(own_tiles.shape),
                whole(other_tiles.shape),
                whole(place.shape),
                whole(first.shape),
                whole(second.shape),
                whole(gain.shape),
                whole(shift_rows.shape),
            ],
            out_specs=pl.BlockSpec((1, 1, channels, 2048), lambda s, ids: (0, s, 0, 0)),
            scratch_shapes=[
                pltpu.VMEM((128, 1024), jnp.bfloat16),
                pltpu.VMEM((128, 1024), jnp.float32),
                pltpu.VMEM((288, 1024), jnp.bfloat16),
                pltpu.VMEM((channels, 2048), jnp.float32),
            ],
        ),
        out_shape=jax.ShapeDtypeStruct((1, MAXPIX, channels, 2048), jnp.bfloat16),
        compiler_params=pltpu.CompilerParams(vmem_limit_bytes=56 << 20),
        name="decode",
    )(ids, own_tiles, other_tiles, place, first, second, gain, shift_rows)


def body(
    tokens,
    project_weight,
    noisy_latent,
    final_weight,
    conv_weight,
    norm_gain,
    norm_shift,
    owner_count,
    intersection,
):
    coordinate = {axis: lax.axis_index(axis).astype(jnp.int32) for axis in AXES}
    head = lax.axis_index(SEQ)

    weights = jnp.concatenate([project_weight, shift(project_weight, c=1)])
    weights = weights.transpose(1, 0, 2).reshape(weights.shape[1], -1)

    w = lax.dynamic_slice_in_dim(final_weight, head * HEAD_DIM, HEAD_DIM, axis=0)
    w = w.reshape(HEAD_DIM, LATENT_CH, PATCH).transpose(2, 1, 0).reshape(64, HEAD_DIM)
    noisy = noisy_latent.reshape(-1, LATENT_CH, PATCH).transpose(2, 1, 0).reshape(64, -1)

    rank = lax.axis_index(AXES)
    ends = jnp.cumsum(owner_count, dtype=jnp.int32)
    count = owner_count[rank]
    slots = jnp.minimum(ends[rank] - count + jnp.arange(MAXPIX), intersection.shape[0] - 1)
    wanted = intersection[slots].reshape(-1)
    core = (wanted // 8) % 2
    wanted = (wanted // 16) * 8 + wanted % 8 + 64 * (core != coordinate["c"])
    ids = jnp.concatenate([count[None], wanted]).astype(jnp.int32)

    taps = conv_weight.astype(jnp.float32).reshape(3, -1, conv_weight.shape[1])
    first = (taps[0] + taps[1] + taps[2]).T.astype(jnp.bfloat16)
    second = jnp.concatenate([taps[0] + taps[1], taps[2]], axis=0).T.astype(jnp.bfloat16)
    placing = jnp.asarray(placing_matrix(), jnp.bfloat16)
    decoder = [first, second, norm_gain[:, None], norm_shift[:, None]]

    half = tokens.shape[0] // 2
    b_own = tokens[half:]
    b_pair = jnp.concatenate([b_own, shift(b_own, xh=1)])
    a_z = lax.all_gather(tokens[:half], "z", axis=0, tiled=True)
    a_x = shift(a_z, xh=1)
    b_all = lax.all_gather(b_pair, "z", axis=0, tiled=True)

    q_scale = LOG2E * HEAD_DIM**-0.5

    def both_cores(own, other):
        return jnp.concatenate([own, shift(other, c=1)])

    q1, kv1, q1_sent, kv1_sent = project([a_z], weights, q_scale)
    q1, kv1 = both_cores(q1, q1_sent), both_cores(kv1, kv1_sent)
    kv1_y = {n: shift(kv1, y=n) for n in (1, 3, 2)}
    done_before = [q1, *kv1_y.values(), ids, w, noisy, *decoder]
    q2, kv2, q2_sent, kv2_sent = project([a_x, b_all], weights, q_scale, done_before)
    kv2 = both_cores(kv2, kv2_sent)
    kv2_y = {n: shift(kv2, y=n) for n in (1, 3, 2)}

    q1 = q1.reshape(1, 2, 4, half, HEAD_DIM)
    q2 = both_cores(q2, q2_sent).reshape(2, 12 * half, HEAD_DIM)
    q_a = jnp.concatenate([q1, q2[:, : 4 * half].reshape(1, 2, 4, half, HEAD_DIM)])
    q_b = q2[:, 4 * half :].reshape(2, 4, 2, half, HEAD_DIM).transpose(2, 0, 1, 3, 4)
    q_own = jnp.concatenate([q_a, q_b], axis=3).reshape(-1, HEAD_DIM)
    q_other = shift(q_own, xl=1)

    early = [kv1, kv2, kv1_y[1], kv1_y[3], kv1_y[2]]
    q_both = jnp.concatenate([q_own, q_other])
    carry = attention(q_own, early, rows_out=q_both.shape[0])
    carry = attention(q_other, early, into=carry)
    place = jnp.stack([coordinate["xl"], coordinate["xh"], coordinate["c"]])
    parts = attention(q_both, [kv2_y[1], kv2_y[3], kv2_y[2]], carry, last=(place, w))
    parts = parts.reshape(-1, PAYLOAD, 128)
    parts = lax.all_to_all(parts, SEQ + ("xl",), split_axis=0, concat_axis=0, tiled=True)
    tile = combine(parts, noisy, 64)

    own_tiles = lax.all_to_all(tile, ("xh", "z", "y", "xl"), split_axis=0, concat_axis=0, tiled=True)
    other_tiles = shift(own_tiles, c=1)
    return decode(ids, own_tiles, other_tiles, placing, *decoder)


def solution(mesh):
    fine = Mesh(mesh.devices.reshape(SIZES), AXES)
    blk = ("y", "xl")
    return jax.shard_map(
        body,
        mesh=fine,
        in_specs=(
            P(SEQ + blk, None),
            P(None, None, SEQ),
            P(SEQ + blk, None),
            P(),
            P(),
            P(),
            P(),
            P(),
            P(),
        ),
        out_specs=P(SEQ + blk, None, None, None),
        check_vma=False,
    )
```

```python
import functools

import jax
import jax.numpy as jnp
import numpy as np
from jax import lax
from jax.experimental import pallas as pl
from jax.experimental.pallas import tpu as pltpu
from jax.sharding import Mesh
from jax.sharding import PartitionSpec as P

HEAD_DIM = 128
LATENT_CH = 16
PATCH = 4
GROUPS = 32
MAXPIX = 4

scale_factor = 0.476986
step_size = 0.25
norm_eps = 1e-06

AXES = ("xh", "z", "c", "y", "xl")
SIZES = (2, 4, 2, 4, 2)
SEQ = ("xh", "z", "c")

NT = (((1,), (1,)), ((), ()))
LOG2E = 1.4426950408889634
PAYLOAD = 80


def shift(x, **moves):
    pairs = []
    for source in range(int(np.prod(SIZES))):
        place = np.unravel_index(source, SIZES)
        target = [(p + moves.get(a, 0)) % n for p, a, n in zip(place, AXES, SIZES)]
        pairs.append((source, int(np.ravel_multi_index(target, SIZES))))
    return lax.ppermute(x, AXES, pairs)


def regroup_kernel(places, n_after, *refs):
    in_refs, out_refs = refs[: len(places)], refs[len(places) + n_after :]
    for in_ref, (out, target) in zip(in_refs, places):
        out_refs[out][target : target + in_ref.shape[0], :] = in_ref[...]


def regroup(groups, after=(), small=(), block=32):
    operands, in_specs, places, shapes = [], [], [], []
    for out, pieces in enumerate(groups):
        target = 0
        for x, start, rows, *columns in pieces:
            column, width = columns or (0, x.shape[1])
            for row in range(start, start + rows, block):
                operands.append(x)
                in_specs.append(
                    pl.BlockSpec((block, width), lambda i, n=row // block, c=column: (n, c))
                )
                places.append((out, target))
                target += block
        shapes.append(jax.ShapeDtypeStruct((target, width), pieces[0][0].dtype))
    return pl.pallas_call(
        functools.partial(regroup_kernel, places, len(after) + len(small)),
        grid=(1,),
        in_specs=in_specs
        + [pl.BlockSpec(memory_space=pltpu.HBM)] * len(after)
        + [pl.BlockSpec(memory_space=pltpu.VMEM)] * len(small),
        out_specs=[pl.BlockSpec(shape.shape, lambda i: (0, 0)) for shape in shapes],
        out_shape=shapes,
        compiler_params=pltpu.CompilerParams(vmem_limit_bytes=20 << 20),
        name="regroup",
    )(*operands, *after, *small)


def project_kernel(q_order, scale, n_after, *refs):
    sources, (own_w_ref, other_w_ref, *refs) = refs[:4], refs[4:]
    q_ref, kv_ref, sent_ref, x_ref, w_ref, sem = refs[n_after:]
    rows = sources[0].shape[0]
    copies = [
        pltpu.make_async_copy(ref, x_ref.at[pl.ds(n * rows, rows), :], sem.at[n])
        for n, ref in enumerate(sources)
    ]
    for copy in copies:
        copy.start()
    for i in range(3):
        for n, weights in enumerate((own_w_ref, other_w_ref)):
            column = (3 * n + i) * HEAD_DIM
            w_ref[:, column : column + HEAD_DIM] = weights[i]
    for first in range(0, 4 * rows, 2 * rows):
        for copy in copies[first // rows : first // rows + 2]:
            copy.wait()
        out = jnp.dot(
            x_ref[first : first + 2 * rows, :], w_ref[...], preferred_element_type=jnp.float32
        )
        own_q = (out[:, :HEAD_DIM] * scale).astype(jnp.bfloat16)
        sent_q = (out[:, 3 * HEAD_DIM : 4 * HEAD_DIM] * scale).astype(jnp.bfloat16)
        for start, count, target in q_order:
            if first <= start < first + 2 * rows:
                piece, target = slice(start - first, start - first + count), slice(target, target + count)
                q_ref[target, :] = own_q[piece]
                sent_ref[target, 2 * HEAD_DIM :] = sent_q[piece]
        piece = slice(first, first + 2 * rows)
        kv_ref[piece, :] = out[:, HEAD_DIM : 3 * HEAD_DIM].astype(jnp.bfloat16)
        sent_ref[piece, : 2 * HEAD_DIM] = out[:, 4 * HEAD_DIM :].astype(jnp.bfloat16)


def project(xs, own_weight, other_weight, q_order, scale, after=()):
    rows, depth = 4 * xs[0].shape[0], own_weight.shape[1]
    widths = [HEAD_DIM, 2 * HEAD_DIM, 3 * HEAD_DIM]
    anywhere, vmem = pl.BlockSpec(memory_space=pltpu.HBM), pl.BlockSpec(memory_space=pltpu.VMEM)
    return pl.pallas_call(
        functools.partial(project_kernel, q_order, scale, len(after)),
        in_specs=[anywhere] * 4 + [vmem] * 2 + [anywhere] * len(after),
        out_specs=[vmem] * 3,
        out_shape=[jax.ShapeDtypeStruct((rows, width), jnp.bfloat16) for width in widths],
        scratch_shapes=[
            pltpu.VMEM((rows, depth), jnp.bfloat16),
            pltpu.VMEM((depth, 6 * HEAD_DIM), jnp.bfloat16),
            pltpu.SemaphoreType.DMA((4,)),
        ],
        compiler_params=pltpu.CompilerParams(vmem_limit_bytes=40 << 20),
        name="project",
    )(*xs, own_weight, other_weight, *after)


def softmax_blocks(q, kv_refs, value_ref, bk, run_max, acc):
    places, start = [], 0
    for ref in kv_refs:
        for i in range(0, ref.shape[0], bk):
            places.append((ref, i, start + i))
        start += ref.shape[0]

    def scores_of(n):
        ref, i, _ = places[n]
        return lax.dot_general(
            q, ref[i : i + bk, :HEAD_DIM], NT, preferred_element_type=jnp.float32
        )

    following = scores_of(0)
    for n, (_, _, row) in enumerate(places):
        scores = following
        if n + 1 < len(places):
            following = scores_of(n + 1)
        new_max = jnp.max(scores, axis=1, keepdims=True)
        if run_max is not None:
            new_max = jnp.maximum(run_max, new_max)
        probs = jnp.exp2(scores - new_max).astype(jnp.bfloat16)
        part = jnp.dot(probs, value_ref[row : row + bk, :], preferred_element_type=jnp.float32)
        acc = part if acc is None else acc * jnp.exp2(run_max - new_max) + part
        run_max = new_max
    return run_max, acc


def attention_kernel(bk, n_q, n_kv, carry_in, n_into, final, *refs):
    if final:
        place_ref, *refs = refs
    q_refs, refs = refs[:n_q], refs[n_q:]
    kv_refs, refs = refs[:n_kv], refs[n_kv:]
    if carry_in:
        acc_in_ref, max_in_ref, *refs = refs
    refs = refs[n_into:]
    if final:
        w_ref, out_ref, value_ref = refs
    else:
        acc_out_ref, max_out_ref, value_ref = refs

    @pl.when(pl.program_id(0) == 0)
    def _():
        start = 0
        for ref in kv_refs:
            n = ref.shape[0]
            value_ref[start : start + n, :HEAD_DIM] = ref[:, HEAD_DIM:]
            value_ref[start : start + n, HEAD_DIM:] = jnp.ones((n, HEAD_DIM), jnp.bfloat16)
            start += n

    q = q_refs[0][...]
    for n in range(1, n_q):
        q = jnp.where(pl.program_id(0) == n, q_refs[n][...], q)
    bq = q.shape[0]
    run_max, acc = None, None
    if carry_in:
        run_max, acc = jnp.max(max_in_ref[...], axis=1, keepdims=True), acc_in_ref[...]
    run_max, acc = softmax_blocks(q, kv_refs, value_ref, bk, run_max, acc)
    if not final:
        acc_out_ref[...] = acc
        max_out_ref[...] = jnp.broadcast_to(run_max, max_out_ref.shape)
        return

    total = acc[:, HEAD_DIM:]
    attended = (acc[:, :HEAD_DIM] / total).astype(jnp.bfloat16)
    velocity = lax.dot_general(w_ref[...], attended, NT, preferred_element_type=jnp.float32)
    log_sum = run_max + jnp.log2(total)
    high = log_sum.astype(jnp.bfloat16).astype(jnp.float32)
    mid = (log_sum - high).astype(jnp.bfloat16).astype(jnp.float32)
    low = log_sum - high - mid
    lane = lax.broadcasted_iota(jnp.int32, (bq, HEAD_DIM), 1)
    terms = jnp.where(lane == 0, high, jnp.where(lane == 1, mid, low)).astype(jnp.bfloat16)
    row = lax.broadcasted_iota(jnp.int32, (PAYLOAD - 64, HEAD_DIM), 0)
    column = lax.broadcasted_iota(jnp.int32, (PAYLOAD - 64, HEAD_DIM), 1)
    pick = ((row == column) & (row < 3)).astype(jnp.float32).astype(jnp.bfloat16)
    stats = lax.dot_general(pick, terms, NT, preferred_element_type=jnp.float32)
    joined = jnp.concatenate([velocity, stats], axis=0).astype(jnp.bfloat16)
    n_xh, n_z, n_c = out_ref.shape[:3]
    late = pl.program_id(0) % 2
    for core in range(n_c):
        for group, (early_place, late_place) in enumerate(zip(*GROUP_PLACES)):
            t = core * len(GROUP_PLACES[0]) + group
            xh, z = [jnp.where(late == 1, q, p) for p, q in zip(early_place, late_place)]
            out_ref[
                (xh + place_ref[1]) % n_xh, (z + place_ref[2]) % n_z, (core + place_ref[3]) % n_c, 0
            ] = joined[:, t * 128 : (t + 1) * 128]


GROUP_PLACES = (((0, 0), (0, 3), (0, 1), (1, 0)), ((0, 2), (1, 3), (1, 1), (1, 2)))


def attention(qs, kvs, carry=None, fresh=False, blocks=(1, 0), last=None, bk=512):
    bq = qs[0].shape[0]
    length = sum(kv.shape[0] for kv in kvs)
    stride, offset = blocks
    widths = (2 * HEAD_DIM, HEAD_DIM)
    whole = lambda x: pl.BlockSpec(x.shape, lambda i, *p: (0, 0))
    carried = [
        pl.BlockSpec((bq, width), lambda i, *p: (i * stride + offset, 0)) for width in widths
    ]
    operands = [*qs, *kvs]
    in_specs = [whole(x) for x in operands]
    aliases = {}
    if carry is not None:
        if last is None:
            aliases = {len(operands): 0, len(operands) + 1: 1}
        operands += carry
        in_specs += [pl.BlockSpec(memory_space=pltpu.HBM)] * 2 if fresh else carried
    if last is None:
        prefetch = []
        out_specs = carried
        out_shape = [jax.ShapeDtypeStruct((4 * bq, width), jnp.float32) for width in widths]
    else:
        prefetch = [last[0]]
        operands.append(last[1])
        in_specs.append(whole(last[1]))
        out_specs = pl.BlockSpec(
            (2, 4, 2, 1, PAYLOAD, 128), lambda i, p: (0, 0, 0, (i // 2 + p[0]) % 2, 0, 0)
        )
        out_shape = jax.ShapeDtypeStruct((2, 4, 2, 2, PAYLOAD, 128), jnp.bfloat16)
    read = carry is not None and not fresh
    return pl.pallas_call(
        functools.partial(
            attention_kernel, bk, len(qs), len(kvs), read, len(aliases) if fresh else 0, last is not None
        ),
        grid_spec=pltpu.PrefetchScalarGridSpec(
            num_scalar_prefetch=len(prefetch),
            grid=(len(qs),),
            in_specs=in_specs,
            out_specs=out_specs,
            scratch_shapes=[pltpu.VMEM((length, 2 * HEAD_DIM), jnp.bfloat16)],
        ),
        out_shape=out_shape,
        input_output_aliases=aliases,
        compiler_params=pltpu.CompilerParams(vmem_limit_bytes=56 << 20),
        name="attention",
    )(*prefetch, *operands)


def combine_kernel(parts_ref, noisy_ref, out_ref):
    velocity = jnp.zeros((64, 128), jnp.float32)
    for head in range(parts_ref.shape[0] // 2):
        logs = []
        for half in range(2):
            terms = parts_ref[2 * head + half, 64:PAYLOAD, :].astype(jnp.float32)
            logs.append(terms[0:1] + terms[1:2] + terms[2:3])
        top = jnp.maximum(logs[0], logs[1])
        first, second = jnp.exp2(logs[0] - top), jnp.exp2(logs[1] - top)
        inverse = 1.0 / (first + second)
        velocity += parts_ref[2 * head, 0:64, :].astype(jnp.float32) * (first * inverse)
        velocity += parts_ref[2 * head + 1, 0:64, :].astype(jnp.float32) * (second * inverse)
    latent = (noisy_ref[...] - step_size * velocity) / scale_factor
    latent = latent.astype(jnp.bfloat16)
    for n in range(out_ref.shape[0]):
        out_ref[n] = latent


def combine(parts, noisy, copies):
    return pl.pallas_call(
        combine_kernel,
        out_shape=jax.ShapeDtypeStruct((copies, 64, 128), jnp.bfloat16),
        name="latent_tile",
    )(parts, noisy)


def placing_matrix():
    side, p, q, f, i, j = np.meshgrid(*[np.arange(n) for n in (2, 2, 2, 2, 8, 8)], indexing="ij")
    target = f * 512 + (2 * i + p) * 32 + side * 16 + 2 * j + q
    place = np.zeros((1024, 1024), np.float32)
    place[np.arange(1024), target.reshape(-1)] = 1.0
    return place


def decode_kernel(
    ids_ref, own_ref, other_ref, place_ref, first_ref, second_ref, gain_ref, shift_ref, out_ref, wide_ref, half_ref, patch_ref, conv_ref, part_ref, mean_ref, scale_ref
):
    slot = pl.program_id(0)

    @pl.when(slot == 0)
    def _():
        for s in range(MAXPIX):
            for half in range(2):
                for side in range(2):
                    n = ids_ref[1 + s * 4 + half * 2 + side]
                    tile = jnp.where(n < 64, own_ref[n % 64], other_ref[n % 64])
                    for pq in range(4):
                        column = (side * 4 + pq) * 128
                        row = (s * 2 + half) * 16
                        wide_ref[row : row + 16, column : column + 128] = tile[pq * 16 : pq * 16 + 16, :]
        half_ref[...] = jnp.dot(wide_ref[...], place_ref[...], preferred_element_type=jnp.float32)

    @pl.when(slot >= ids_ref[0])
    def _():
        out_ref[...] = jnp.zeros(out_ref.shape, out_ref.dtype)

    @pl.when(slot < ids_ref[0])
    def _():
        start = pl.multiple_of(slot * 32, 32)
        both = half_ref[pl.ds(start, 32), :]
        frames = []
        for f in range(2):
            frames.append(
                jnp.concatenate(
                    [both[0:16, f * 512 : f * 512 + 512], both[16:32, f * 512 : f * 512 + 512]], axis=1
                )
            )
        region = jnp.concatenate(frames, axis=0)
        lane = lax.broadcasted_iota(jnp.int32, region.shape, 1)
        column = lane % 32
        for g in range(3):
            if g == 0:
                across = jnp.where(column == 0, region, pltpu.roll(region, 1, 1))
            elif g == 1:
                across = region
            else:
                across = jnp.where(column == 31, region, pltpu.roll(region, 1023, 1))
            for b in range(3):
                if b == 0:
                    tap = jnp.where(lane < 32, across, pltpu.roll(across, 32, 1))
                elif b == 1:
                    tap = across
                else:
                    tap = jnp.where(lane >= 992, across, pltpu.roll(across, 992, 1))
                row = (b * 3 + g) * 16
                tap = tap.astype(jnp.bfloat16)
                patch_ref[row : row + 16, :] = tap[0:16]
                patch_ref[144 + row : 144 + row + 16, :] = tap[16:32]
        conv_ref[:, :1024] = jnp.dot(
            first_ref[...], patch_ref[0:144, :], preferred_element_type=jnp.float32
        )
        conv_ref[:, 1024:] = jnp.dot(
            second_ref[...], patch_ref[...], preferred_element_type=jnp.float32
        )
        channels, voxels = conv_ref.shape
        size = channels // GROUPS
        count = 1.0 / (size * voxels)

        def group_rows(group):
            return slice(group * size, (group + 1) * size)

        def group_means():
            sums = jnp.sum(part_ref[...], axis=1, keepdims=True)
            sums = jnp.sum(sums.reshape(GROUPS, 8, 1), axis=1, keepdims=True) * count
            return jnp.broadcast_to(sums, (GROUPS, size, 128)).reshape(channels, 128)

        for group in range(GROUPS):
            total = jnp.zeros((size, 128), jnp.float32)
            for j in range(0, voxels, 128):
                total += conv_ref[group_rows(group), j : j + 128]
            part_ref[group * 8 : group * 8 + 8, :] = total[:8] + total[8:]
        mean_ref[...] = group_means()
        for group in range(GROUPS):
            mean = mean_ref[group_rows(group), :]
            total = jnp.zeros((size, 128), jnp.float32)
            for j in range(0, voxels, 128):
                apart = conv_ref[group_rows(group), j : j + 128] - mean
                total += apart * apart
            part_ref[group * 8 : group * 8 + 8, :] = total[:8] + total[8:]
        scale_ref[...] = gain_ref[...] * (lax.rsqrt(group_means() + norm_eps) * 0.5)
        for group in range(GROUPS):
            rows = group_rows(group)
            mean, scale = mean_ref[rows, :], scale_ref[rows, :]
            half_shift = jnp.broadcast_to(shift_ref[rows, :] * 0.5, (size, 128))
            for j in range(0, voxels, 128):
                half_norm = (conv_ref[rows, j : j + 128] - mean) * scale + half_shift
                out_ref[0, 0, rows, j : j + 128] = (
                    half_norm + half_norm * jnp.tanh(half_norm)
                ).astype(jnp.bfloat16)


def decode(ids, own_tiles, other_tiles, place, first, second, gain, shift_rows):
    channels = first.shape[0]
    whole = lambda shape: pl.BlockSpec(shape, lambda s, ids: (0,) * len(shape))
    return pl.pallas_call(
        decode_kernel,
        grid_spec=pltpu.PrefetchScalarGridSpec(
            num_scalar_prefetch=1,
            grid=(MAXPIX,),
            in_specs=[
                whole(own_tiles.shape),
                whole(other_tiles.shape),
                whole(place.shape),
                whole(first.shape),
                whole(second.shape),
                whole(gain.shape),
                whole(shift_rows.shape),
            ],
            out_specs=pl.BlockSpec((1, 1, channels, 2048), lambda s, ids: (0, s, 0, 0)),
            scratch_shapes=[
                pltpu.VMEM((128, 1024), jnp.bfloat16),
                pltpu.VMEM((128, 1024), jnp.float32),
                pltpu.VMEM((288, 1024), jnp.bfloat16),
                pltpu.VMEM((channels, 2048), jnp.float32),
                pltpu.VMEM((GROUPS * 8, 128), jnp.float32),
                pltpu.VMEM((channels, 128), jnp.float32),
                pltpu.VMEM((channels, 128), jnp.float32),
            ],
        ),
        out_shape=jax.ShapeDtypeStruct((1, MAXPIX, channels, 2048), jnp.bfloat16),
        compiler_params=pltpu.CompilerParams(vmem_limit_bytes=56 << 20),
        name="decode",
    )(ids, own_tiles, other_tiles, place, first, second, gain, shift_rows)


def body(
    tokens,
    project_weight,
    noisy_latent,
    final_weight,
    conv_weight,
    norm_gain,
    norm_shift,
    owner_count,
    intersection,
):
    coordinate = {axis: lax.axis_index(axis).astype(jnp.int32) for axis in AXES}
    head = lax.axis_index(SEQ)

    w = lax.dynamic_slice_in_dim(final_weight, head * HEAD_DIM, HEAD_DIM, axis=0)
    w = w.reshape(HEAD_DIM, LATENT_CH, PATCH).transpose(2, 1, 0).reshape(64, HEAD_DIM)
    noisy = noisy_latent.reshape(-1, LATENT_CH, PATCH).transpose(2, 1, 0).reshape(64, -1)

    rank = lax.axis_index(AXES)
    ends = jnp.cumsum(owner_count, dtype=jnp.int32)
    count = owner_count[rank]
    slots = jnp.minimum(ends[rank] - count + jnp.arange(MAXPIX), intersection.shape[0] - 1)
    wanted = intersection[slots].reshape(-1)
    core = (wanted // 8) % 2
    wanted = (wanted // 16) * 8 + wanted % 8 + 64 * (core != coordinate["c"])
    ids = jnp.concatenate([count[None], wanted]).astype(jnp.int32)

    taps = conv_weight.astype(jnp.float32).reshape(3, -1, conv_weight.shape[1])
    first = (taps[0] + taps[1] + taps[2]).T.astype(jnp.bfloat16)
    second = jnp.concatenate([taps[0] + taps[1], taps[2]], axis=0).T.astype(jnp.bfloat16)
    placing = jnp.asarray(placing_matrix(), jnp.bfloat16)
    decoder = [first, second, norm_gain[:, None], norm_shift[:, None]]

    other_weight = shift(project_weight, c=1)
    below, above, across = shift(tokens, z=1), shift(tokens, z=-1), shift(tokens, xh=1)
    opposite = shift(tokens, xh=1, z=2)
    to_above, to_below, to_across = regroup(
        [
            [(below, 0, 64), (across, 0, 32), (across, 96, 32)],
            [(across, 0, 32), (across, 96, 32), (above, 64, 64)],
            [(below, 32, 64), (above, 32, 64)],
        ],
        small=decoder[:2],
    )
    far_low, far_high, inner = shift(to_above, z=1), shift(to_below, z=-1), shift(to_across, xh=1)

    q_scale = LOG2E * HEAD_DIM**-0.5

    def join(own, received, column, width, after=(), small=()):
        rows = own.shape[0]
        pieces = [(own, 0, rows), (received, 0, rows, column, width)]
        return regroup([pieces], after, small, block=rows)[0]

    early = [tokens, below, above, across]
    early = project(early, project_weight, other_weight, [(0, 256, 0), (256, 256, 256)], q_scale, [to_above])
    received = shift(early[2], c=1)
    kv1 = [join(early[1], received, 0, 2 * HEAD_DIM)]
    kv1 += [shift(kv1[0], y=1), shift(kv1[0], y=3)]
    arrived = [*kv1[1:], far_low, far_high, inner, opposite]
    q1 = join(early[0], received, 2, HEAD_DIM, arrived, [ids, w, noisy, *decoder[2:]])
    kv1_again = join(early[1], received, 0, 2 * HEAD_DIM, after=arrived)
    prepared = [q1, kv1_again]
    kv1.append(shift(kv1_again, y=2))
    q1 = [q1, shift(q1, xl=1)]

    late_order = [(0, 64, 0), (64, 32, 128), (96, 32, 224)]
    late_order += [(128, 32, 256), (160, 32, 352), (192, 64, 64)]
    late_order += [(256, 64, 160), (320, 64, 288), (384, 128, 384)]
    late = [far_low, far_high, inner, opposite]
    q2, own_kv2, sent = project(late, project_weight, other_weight, late_order, q_scale, prepared)
    received = shift(sent, c=1)
    kv2 = [join(own_kv2, received, 0, 2 * HEAD_DIM)]
    kv2 += [shift(kv2[0], y=n) for n in (1, 3, 2)]
    q2 = join(q2, received, 2, HEAD_DIM)
    q2 = [q2, shift(q2, xl=1)]

    carry = attention(q1, [*kv1[:3], kv2[0]], blocks=(2, 0))
    carry = attention(q2, [*kv1[:3], kv2[0]], carry, fresh=True, blocks=(2, 1))
    q_all = [q1[0], q2[0], q1[1], q2[1]]
    place = jnp.stack([coordinate[axis] for axis in ("xl", "xh", "z", "c")])
    parts = attention(q_all, [kv1[3], *kv2[1:]], carry, last=(place, w))
    parts = parts.reshape(-1, PAYLOAD, 128)
    parts = lax.all_to_all(parts, SEQ + ("xl",), split_axis=0, concat_axis=0, tiled=True)
    tile = combine(parts, noisy, 64)

    own_tiles = lax.all_to_all(tile, ("xh", "z", "y", "xl"), split_axis=0, concat_axis=0, tiled=True)
    other_tiles = shift(own_tiles, c=1)
    return decode(ids, own_tiles, other_tiles, placing, *decoder)


def solution(mesh):
    fine = Mesh(mesh.devices.reshape(SIZES), AXES)
    blk = ("y", "xl")
    return jax.shard_map(
        body,
        mesh=fine,
        in_specs=(
            P(SEQ + blk, None),
            P(None, None, SEQ),
            P(SEQ + blk, None),
            P(),
            P(),
            P(),
            P(),
            P(),
            P(),
        ),
        out_specs=P(SEQ + blk, None, None, None),
        check_vma=False,
    )
```

```python
import functools

import jax
import jax.numpy as jnp
import numpy as np
from jax import lax
from jax.experimental import pallas as pl
from jax.experimental.pallas import tpu as pltpu
from jax.sharding import Mesh
from jax.sharding import PartitionSpec as P

HEAD_DIM = 128
LATENT_CH = 16
PATCH = 4
GROUPS = 32
MAXPIX = 4
PARTS = 2

scale_factor = 0.476986
step_size = 0.25
norm_eps = 1e-06

AXES = ("xh", "z", "c", "y", "xl")
SIZES = (2, 4, 2, 4, 2)
SEQ = ("xh", "z", "c")

NT = (((1,), (1,)), ((), ()))
LOG2E = 1.4426950408889634
PAYLOAD = 80


def shift(x, **moves):
    pairs = []
    for source in range(int(np.prod(SIZES))):
        place = np.unravel_index(source, SIZES)
        target = [(p + moves.get(a, 0)) % n for p, a, n in zip(place, AXES, SIZES)]
        pairs.append((source, int(np.ravel_multi_index(target, SIZES))))
    return lax.ppermute(x, AXES, pairs)


def regroup_kernel(places, n_after, *refs):
    in_refs, out_refs = refs[: len(places)], refs[len(places) + n_after :]
    for in_ref, (out, target) in zip(in_refs, places):
        out_refs[out][target : target + in_ref.shape[0], :] = in_ref[...]


def regroup(groups, after=(), small=(), block=32):
    operands, in_specs, places, shapes = [], [], [], []
    for out, pieces in enumerate(groups):
        target = 0
        for x, start, rows, *columns in pieces:
            column, width = columns or (0, x.shape[1])
            for row in range(start, start + rows, block):
                operands.append(x)
                in_specs.append(
                    pl.BlockSpec((block, width), lambda i, n=row // block, c=column: (n, c))
                )
                places.append((out, target))
                target += block
        shapes.append(jax.ShapeDtypeStruct((target, width), pieces[0][0].dtype))
    return pl.pallas_call(
        functools.partial(regroup_kernel, places, len(after) + len(small)),
        grid=(1,),
        in_specs=in_specs
        + [pl.BlockSpec(memory_space=pltpu.HBM)] * len(after)
        + [pl.BlockSpec(memory_space=pltpu.VMEM)] * len(small),
        out_specs=[pl.BlockSpec(shape.shape, lambda i: (0, 0)) for shape in shapes],
        out_shape=shapes,
        compiler_params=pltpu.CompilerParams(vmem_limit_bytes=20 << 20),
        name="regroup",
    )(*operands, *after, *small)


def project_kernel(q_order, scale, n_after, *refs):
    sources, (own_w_ref, other_w_ref, *refs) = refs[:4], refs[4:]
    q_ref, kv_ref, sent_ref, x_ref, w_ref, sem = refs[n_after:]
    rows = sources[0].shape[0]
    copies = [
        pltpu.make_async_copy(ref, x_ref.at[pl.ds(n * rows, rows), :], sem.at[n])
        for n, ref in enumerate(sources)
    ]
    for copy in copies:
        copy.start()
    for i in range(3):
        for n, weights in enumerate((own_w_ref, other_w_ref)):
            column = (3 * n + i) * HEAD_DIM
            w_ref[:, column : column + HEAD_DIM] = weights[i]
    for first in range(0, 4 * rows, 2 * rows):
        for copy in copies[first // rows : first // rows + 2]:
            copy.wait()
        out = jnp.dot(
            x_ref[first : first + 2 * rows, :], w_ref[...], preferred_element_type=jnp.float32
        )
        own_q = (out[:, :HEAD_DIM] * scale).astype(jnp.bfloat16)
        sent_q = (out[:, 3 * HEAD_DIM : 4 * HEAD_DIM] * scale).astype(jnp.bfloat16)
        for start, count, target in q_order:
            if first <= start < first + 2 * rows:
                piece, target = slice(start - first, start - first + count), slice(target, target + count)
                q_ref[target, :] = own_q[piece]
                sent_ref[target, 2 * HEAD_DIM :] = sent_q[piece]
        piece = slice(first, first + 2 * rows)
        kv_ref[piece, :] = out[:, HEAD_DIM : 3 * HEAD_DIM].astype(jnp.bfloat16)
        sent_ref[piece, : 2 * HEAD_DIM] = out[:, 4 * HEAD_DIM :].astype(jnp.bfloat16)


def project(xs, own_weight, other_weight, q_order, scale, after=()):
    rows, depth = 4 * xs[0].shape[0], own_weight.shape[1]
    widths = [HEAD_DIM, 2 * HEAD_DIM, 3 * HEAD_DIM]
    anywhere, vmem = pl.BlockSpec(memory_space=pltpu.HBM), pl.BlockSpec(memory_space=pltpu.VMEM)
    return pl.pallas_call(
        functools.partial(project_kernel, q_order, scale, len(after)),
        in_specs=[anywhere] * 4 + [vmem] * 2 + [anywhere] * len(after),
        out_specs=[vmem] * 3,
        out_shape=[jax.ShapeDtypeStruct((rows, width), jnp.bfloat16) for width in widths],
        scratch_shapes=[
            pltpu.VMEM((rows, depth), jnp.bfloat16),
            pltpu.VMEM((depth, 6 * HEAD_DIM), jnp.bfloat16),
            pltpu.SemaphoreType.DMA((4,)),
        ],
        compiler_params=pltpu.CompilerParams(vmem_limit_bytes=40 << 20),
        name="project",
    )(*xs, own_weight, other_weight, *after)


def softmax_blocks(q, kv_refs, value_ref, bk, run_max, acc):
    places, start = [], 0
    for ref in kv_refs:
        for i in range(0, ref.shape[0], bk):
            places.append((ref, i, start + i))
        start += ref.shape[0]

    def scores_of(n):
        ref, i, _ = places[n]
        return lax.dot_general(
            q, ref[i : i + bk, :HEAD_DIM], NT, preferred_element_type=jnp.float32
        )

    following = scores_of(0)
    for n, (_, _, row) in enumerate(places):
        scores = following
        if n + 1 < len(places):
            following = scores_of(n + 1)
        new_max = jnp.max(scores, axis=1, keepdims=True)
        if run_max is not None:
            new_max = jnp.maximum(run_max, new_max)
        probs = jnp.exp2(scores - new_max).astype(jnp.bfloat16)
        part = jnp.dot(probs, value_ref[row : row + bk, :], preferred_element_type=jnp.float32)
        acc = part if acc is None else acc * jnp.exp2(run_max - new_max) + part
        run_max = new_max
    return run_max, acc


def attention_kernel(bk, n_q, n_kv, carry_in, n_into, final, *refs):
    if final:
        place_ref, *refs = refs
    q_refs, refs = refs[:n_q], refs[n_q:]
    kv_refs, refs = refs[:n_kv], refs[n_kv:]
    if carry_in:
        acc_in_ref, max_in_ref, *refs = refs
    refs = refs[n_into:]
    if final:
        w_ref, out_ref, value_ref = refs
    else:
        acc_out_ref, max_out_ref, value_ref = refs

    @pl.when(pl.program_id(0) == 0)
    def _():
        start = 0
        for ref in kv_refs:
            n = ref.shape[0]
            value_ref[start : start + n, :HEAD_DIM] = ref[:, HEAD_DIM:]
            value_ref[start : start + n, HEAD_DIM:] = jnp.ones((n, HEAD_DIM), jnp.bfloat16)
            start += n

    q = q_refs[0][...]
    for n in range(1, n_q):
        q = jnp.where(pl.program_id(0) == n, q_refs[n][...], q)
    bq = q.shape[0]
    run_max, acc = None, None
    if carry_in:
        run_max, acc = jnp.max(max_in_ref[...], axis=1, keepdims=True), acc_in_ref[...]
    run_max, acc = softmax_blocks(q, kv_refs, value_ref, bk, run_max, acc)
    if not final:
        acc_out_ref[...] = acc
        max_out_ref[...] = jnp.broadcast_to(run_max, max_out_ref.shape)
        return

    total = acc[:, HEAD_DIM:]
    attended = (acc[:, :HEAD_DIM] / total).astype(jnp.bfloat16)
    velocity = lax.dot_general(w_ref[...], attended, NT, preferred_element_type=jnp.float32)
    log_sum = run_max + jnp.log2(total)
    high = log_sum.astype(jnp.bfloat16).astype(jnp.float32)
    mid = (log_sum - high).astype(jnp.bfloat16).astype(jnp.float32)
    low = log_sum - high - mid
    lane = lax.broadcasted_iota(jnp.int32, (bq, HEAD_DIM), 1)
    terms = jnp.where(lane == 0, high, jnp.where(lane == 1, mid, low)).astype(jnp.bfloat16)
    row = lax.broadcasted_iota(jnp.int32, (PAYLOAD - 64, HEAD_DIM), 0)
    column = lax.broadcasted_iota(jnp.int32, (PAYLOAD - 64, HEAD_DIM), 1)
    pick = ((row == column) & (row < 3)).astype(jnp.float32).astype(jnp.bfloat16)
    stats = lax.dot_general(pick, terms, NT, preferred_element_type=jnp.float32)
    joined = jnp.concatenate([velocity, stats], axis=0).astype(jnp.bfloat16)
    n_xh, n_z, n_c = out_ref.shape[:3]
    late = pl.program_id(0) % 2
    for core in range(n_c):
        for group, (early_place, late_place) in enumerate(zip(*GROUP_PLACES)):
            t = core * len(GROUP_PLACES[0]) + group
            xh, z = [jnp.where(late == 1, q, p) for p, q in zip(early_place, late_place)]
            out_ref[
                (xh + place_ref[1]) % n_xh, (z + place_ref[2]) % n_z, (core + place_ref[3]) % n_c, 0
            ] = joined[:, t * 128 : (t + 1) * 128]


GROUP_PLACES = (((0, 0), (0, 3), (0, 1), (1, 0)), ((0, 2), (1, 3), (1, 1), (1, 2)))


def attention(qs, kvs, carry=None, fresh=False, blocks=(1, 0), last=None, bk=512):
    bq = qs[0].shape[0]
    length = sum(kv.shape[0] for kv in kvs)
    stride, offset = blocks
    widths = (2 * HEAD_DIM, HEAD_DIM)
    whole = lambda x: pl.BlockSpec(x.shape, lambda i, *p: (0, 0))
    carried = [
        pl.BlockSpec((bq, width), lambda i, *p: (i * stride + offset, 0)) for width in widths
    ]
    operands = [*qs, *kvs]
    in_specs = [whole(x) for x in operands]
    aliases = {}
    if carry is not None:
        if last is None:
            aliases = {len(operands): 0, len(operands) + 1: 1}
        operands += carry
        in_specs += [pl.BlockSpec(memory_space=pltpu.HBM)] * 2 if fresh else carried
    if last is None:
        prefetch = []
        out_specs = carried
        out_shape = [jax.ShapeDtypeStruct((4 * bq, width), jnp.float32) for width in widths]
    else:
        prefetch = [last[0]]
        operands.append(last[1])
        in_specs.append(whole(last[1]))
        out_specs = pl.BlockSpec(
            (2, 4, 2, 1, PAYLOAD, 128), lambda i, p: (0, 0, 0, (i // 2 + p[0]) % 2, 0, 0)
        )
        out_shape = jax.ShapeDtypeStruct((2, 4, 2, 2, PAYLOAD, 128), jnp.bfloat16)
    read = carry is not None and not fresh
    return pl.pallas_call(
        functools.partial(
            attention_kernel, bk, len(qs), len(kvs), read, len(aliases) if fresh else 0, last is not None
        ),
        grid_spec=pltpu.PrefetchScalarGridSpec(
            num_scalar_prefetch=len(prefetch),
            grid=(len(qs),),
            in_specs=in_specs,
            out_specs=out_specs,
            scratch_shapes=[pltpu.VMEM((length, 2 * HEAD_DIM), jnp.bfloat16)],
        ),
        out_shape=out_shape,
        input_output_aliases=aliases,
        compiler_params=pltpu.CompilerParams(vmem_limit_bytes=56 << 20),
        name="attention",
    )(*prefetch, *operands)


def combine_kernel(parts_ref, noisy_ref, out_ref):
    velocity = jnp.zeros((64, 128), jnp.float32)
    for head in range(parts_ref.shape[0] // 2):
        logs = []
        for half in range(2):
            terms = parts_ref[2 * head + half, 64:PAYLOAD, :].astype(jnp.float32)
            logs.append(terms[0:1] + terms[1:2] + terms[2:3])
        top = jnp.maximum(logs[0], logs[1])
        first, second = jnp.exp2(logs[0] - top), jnp.exp2(logs[1] - top)
        inverse = 1.0 / (first + second)
        velocity += parts_ref[2 * head, 0:64, :].astype(jnp.float32) * (first * inverse)
        velocity += parts_ref[2 * head + 1, 0:64, :].astype(jnp.float32) * (second * inverse)
    latent = (noisy_ref[...] - step_size * velocity) / scale_factor
    latent = latent.astype(jnp.bfloat16)
    for n in range(out_ref.shape[0]):
        out_ref[n] = latent


def combine(parts, noisy, copies):
    return pl.pallas_call(
        combine_kernel,
        out_shape=jax.ShapeDtypeStruct((copies, 64, 128), jnp.bfloat16),
        name="latent_tile",
    )(parts, noisy)


def placing_matrix():
    side, p, q, i, j = np.meshgrid(*[np.arange(n) for n in (2, 2, 2, 8, 8)], indexing="ij")
    target = (2 * i + p) * 32 + side * 16 + 2 * j + q
    place = np.zeros((512, 512), np.float32)
    place[np.arange(512), target.reshape(-1)] = 1.0
    return place


def decode_kernel(
    ids_ref, own_ref, other_ref, place_ref, first_ref, second_ref, gain_ref, shift_ref, out_ref, wide_ref, half_ref, patch_ref, conv_ref, part_ref, mean_ref, scale_ref, mid_ref
):
    slot, part = pl.program_id(0), pl.program_id(1)
    channels, voxels = conv_ref.shape
    these = pl.ds(pl.multiple_of(part * channels, channels), channels)

    @pl.when((slot == 0) & (part == 0))
    def _():
        for s in range(MAXPIX):
            for half in range(2):
                for side in range(2):
                    n = ids_ref[1 + s * 4 + half * 2 + side]
                    tile = jnp.where(n < 64, own_ref[n % 64], other_ref[n % 64])
                    for pq in range(4):
                        column = (side * 4 + pq) * 64
                        for f in range(2):
                            row = ((s * 2 + f) * 2 + half) * 16
                            wide_ref[row : row + 16, column : column + 64] = tile[
                                pq * 16 : pq * 16 + 16, f * 64 : f * 64 + 64
                            ]
        half_ref[...] = jnp.dot(wide_ref[...], place_ref[...], preferred_element_type=jnp.float32)

    @pl.when(slot >= ids_ref[0])
    def _():
        out_ref[...] = jnp.zeros(out_ref.shape, out_ref.dtype)

    @pl.when((slot < ids_ref[0]) & (part == 0))
    def _():
        halves = half_ref[pl.ds(pl.multiple_of(slot * 64, 64), 64), :]
        region = jnp.concatenate(
            [
                jnp.concatenate([halves[0:16], halves[16:32]], axis=1),
                jnp.concatenate([halves[32:48], halves[48:64]], axis=1),
            ],
            axis=0,
        )
        lane = lax.broadcasted_iota(jnp.int32, region.shape, 1)
        column = lane % 32
        for g in range(3):
            if g == 0:
                across = jnp.where(column == 0, region, pltpu.roll(region, 1, 1))
            elif g == 1:
                across = region
            else:
                across = jnp.where(column == 31, region, pltpu.roll(region, 1023, 1))
            for b in range(3):
                if b == 0:
                    tap = jnp.where(lane < 32, across, pltpu.roll(across, 32, 1))
                elif b == 1:
                    tap = across
                else:
                    tap = jnp.where(lane >= 992, across, pltpu.roll(across, 992, 1))
                row = (b * 3 + g) * 16
                tap = tap.astype(jnp.bfloat16)
                patch_ref[row : row + 16, :] = tap[0:16]
                patch_ref[144 + row : 144 + row + 16, :] = tap[16:32]
    @pl.when(slot < ids_ref[0])
    def _():
        conv_ref[:, :1024] = jnp.dot(
            first_ref[these, :], patch_ref[0:144, :], preferred_element_type=jnp.float32
        )
        conv_ref[:, 1024:] = jnp.dot(
            second_ref[these, :], patch_ref[...], preferred_element_type=jnp.float32
        )
        groups = GROUPS // PARTS
        size = channels // groups
        count = 1.0 / (size * voxels)

        def group_rows(group):
            return slice(group * size, (group + 1) * size)

        def group_means():
            sums = jnp.sum(part_ref[...], axis=1, keepdims=True)
            sums = jnp.sum(sums.reshape(groups, 8, 1), axis=1, keepdims=True) * count
            return jnp.broadcast_to(sums, (groups, size, 128)).reshape(channels, 128)

        for group in range(groups):
            total = jnp.zeros((size, 128), jnp.float32)
            for j in range(0, voxels, 128):
                total += conv_ref[group_rows(group), j : j + 128]
            part_ref[group * 8 : group * 8 + 8, :] = total[:8] + total[8:]
        mean_ref[...] = group_means()
        for group in range(groups):
            mean = mean_ref[group_rows(group), :]
            total = jnp.zeros((size, 128), jnp.float32)
            for j in range(0, voxels, 128):
                apart = conv_ref[group_rows(group), j : j + 128] - mean
                total += apart * apart
            part_ref[group * 8 : group * 8 + 8, :] = total[:8] + total[8:]
        scale_ref[...] = gain_ref[these, :] * (lax.rsqrt(group_means() + norm_eps) * 0.5)
        mid_ref[...] = jnp.broadcast_to(shift_ref[these, :] * 0.5, mid_ref.shape)
        for group in range(groups):
            rows = group_rows(group)
            mean, scale = mean_ref[rows, :], scale_ref[rows, :]
            half_shift = mid_ref[rows, :]
            for j in range(0, voxels, 128):
                half_norm = (conv_ref[rows, j : j + 128] - mean) * scale + half_shift
                out_ref[0, 0, rows, j : j + 128] = (
                    half_norm + half_norm * jnp.tanh(half_norm)
                ).astype(jnp.bfloat16)


def decode(ids, own_tiles, other_tiles, place, first, second, gain, shift_rows):
    channels = first.shape[0]
    whole = lambda shape: pl.BlockSpec(memory_space=pltpu.VMEM)
    rows = channels // PARTS
    return pl.pallas_call(
        decode_kernel,
        grid_spec=pltpu.PrefetchScalarGridSpec(
            num_scalar_prefetch=1,
            grid=(MAXPIX, PARTS),
            in_specs=[
                whole(own_tiles.shape),
                whole(other_tiles.shape),
                whole(place.shape),
                whole(first.shape),
                whole(second.shape),
                whole(gain.shape),
                whole(shift_rows.shape),
            ],
            out_specs=pl.BlockSpec((1, 1, rows, 2048), lambda s, h, ids: (0, s, h, 0)),
            scratch_shapes=[
                pltpu.VMEM((256, 512), jnp.bfloat16),
                pltpu.VMEM((256, 512), jnp.float32),
                pltpu.VMEM((288, 1024), jnp.bfloat16),
                pltpu.VMEM((rows, 2048), jnp.float32),
                pltpu.VMEM((GROUPS // PARTS * 8, 128), jnp.float32),
                pltpu.VMEM((rows, 128), jnp.float32),
                pltpu.VMEM((rows, 128), jnp.float32),
                pltpu.VMEM((rows, 128), jnp.float32),
            ],
        ),
        out_shape=jax.ShapeDtypeStruct((1, MAXPIX, channels, 2048), jnp.bfloat16),
        compiler_params=pltpu.CompilerParams(vmem_limit_bytes=28 << 20),
        name="decode",
    )(ids, own_tiles, other_tiles, place, first, second, gain, shift_rows)


def body(
    tokens,
    project_weight,
    noisy_latent,
    final_weight,
    conv_weight,
    norm_gain,
    norm_shift,
    owner_count,
    intersection,
):
    coordinate = {axis: lax.axis_index(axis).astype(jnp.int32) for axis in AXES}
    head = lax.axis_index(SEQ)

    w = lax.dynamic_slice_in_dim(final_weight, head * HEAD_DIM, HEAD_DIM, axis=0)
    w = w.reshape(HEAD_DIM, LATENT_CH, PATCH).transpose(2, 1, 0).reshape(64, HEAD_DIM)
    noisy = noisy_latent.reshape(-1, LATENT_CH, PATCH).transpose(2, 1, 0).reshape(64, -1)

    rank = lax.axis_index(AXES)
    ends = jnp.cumsum(owner_count, dtype=jnp.int32)
    count = owner_count[rank]
    slots = jnp.minimum(ends[rank] - count + jnp.arange(MAXPIX), intersection.shape[0] - 1)
    wanted = intersection[slots].reshape(-1)
    core = (wanted // 8) % 2
    wanted = (wanted // 16) * 8 + wanted % 8 + 64 * (core != coordinate["c"])
    ids = jnp.concatenate([count[None], wanted]).astype(jnp.int32)

    taps = conv_weight.astype(jnp.float32).reshape(3, -1, conv_weight.shape[1])
    first = (taps[0] + taps[1] + taps[2]).T.astype(jnp.bfloat16)
    second = jnp.concatenate([taps[0] + taps[1], taps[2]], axis=0).T.astype(jnp.bfloat16)
    placing = jnp.asarray(placing_matrix(), jnp.bfloat16)
    decoder = [first, second, norm_gain[:, None], norm_shift[:, None]]

    other_weight = shift(project_weight, c=1)
    below, above, across = shift(tokens, z=1), shift(tokens, z=-1), shift(tokens, xh=1)
    opposite = shift(tokens, xh=1, z=2)
    to_above, to_below, to_across = regroup(
        [
            [(below, 0, 64), (across, 0, 32), (across, 96, 32)],
            [(across, 0, 32), (across, 96, 32), (above, 64, 64)],
            [(below, 32, 64), (above, 32, 64)],
        ],
        small=decoder[:2],
    )
    far_low, far_high, inner = shift(to_above, z=1), shift(to_below, z=-1), shift(to_across, xh=1)

    q_scale = LOG2E * HEAD_DIM**-0.5

    def join(own, received, column, width, after=(), small=()):
        rows = own.shape[0]
        pieces = [(own, 0, rows), (received, 0, rows, column, width)]
        return regroup([pieces], after, small, block=rows)[0]

    early = [tokens, below, above, across]
    early = project(early, project_weight, other_weight, [(0, 256, 0), (256, 256, 256)], q_scale, [to_above])
    received = shift(early[2], c=1)
    kv1 = [join(early[1], received, 0, 2 * HEAD_DIM)]
    kv1 += [shift(kv1[0], y=1), shift(kv1[0], y=3)]
    arrived = [*kv1[1:], far_low, far_high, inner, opposite]
    q1 = join(early[0], received, 2, HEAD_DIM)
    kv1_again = join(early[1], received, 0, 2 * HEAD_DIM, arrived, [ids, w, noisy, *decoder[2:]])
    prepared = [q1, kv1_again]
    kv1.append(shift(kv1_again, y=2))
    q1 = [q1, shift(q1, xl=1)]

    late_order = [(0, 64, 0), (64, 32, 128), (96, 32, 224)]
    late_order += [(128, 32, 256), (160, 32, 352), (192, 64, 64)]
    late_order += [(256, 64, 160), (320, 64, 288), (384, 128, 384)]
    late = [far_low, far_high, inner, opposite]
    q2, own_kv2, sent = project(late, project_weight, other_weight, late_order, q_scale, prepared)
    received = shift(sent, c=1)
    kv2 = [join(own_kv2, received, 0, 2 * HEAD_DIM)]
    kv2 += [shift(kv2[0], y=n) for n in (1, 3, 2)]
    q2 = join(q2, received, 2, HEAD_DIM)
    q2 = [q2, shift(q2, xl=1)]

    carry = attention(q1, [*kv1[:3], kv2[0]], blocks=(2, 0))
    carry = attention(q2, [*kv1[:3], kv2[0]], carry, fresh=True, blocks=(2, 1))
    q_all = [q1[0], q2[0], q1[1], q2[1]]
    place = jnp.stack([coordinate[axis] for axis in ("xl", "xh", "z", "c")])
    parts = attention(q_all, [kv1[3], *kv2[1:]], carry, last=(place, w))
    parts = parts.reshape(-1, PAYLOAD, 128)
    parts = lax.all_to_all(parts, SEQ + ("xl",), split_axis=0, concat_axis=0, tiled=True)
    tile = combine(parts, noisy, 64)

    own_tiles = lax.all_to_all(tile, ("xh", "z", "y", "xl"), split_axis=0, concat_axis=0, tiled=True)
    other_tiles = shift(own_tiles, c=1)
    return decode(ids, own_tiles, other_tiles, placing, *decoder)


def solution(mesh):
    fine = Mesh(mesh.devices.reshape(SIZES), AXES)
    blk = ("y", "xl")
    return jax.shard_map(
        body,
        mesh=fine,
        in_specs=(
            P(SEQ + blk, None),
            P(None, None, SEQ),
            P(SEQ + blk, None),
            P(),
            P(),
            P(),
            P(),
            P(),
            P(),
        ),
        out_specs=P(SEQ + blk, None, None, None),
        check_vma=False,
    )
```

```python
import functools

import jax
import jax.numpy as jnp
import numpy as np
from jax import lax
from jax.experimental import pallas as pl
from jax.experimental.pallas import tpu as pltpu
from jax.sharding import Mesh
from jax.sharding import PartitionSpec as P

HEAD_DIM = 128
LATENT_CH = 16
PATCH = 4
GROUPS = 32
MAXPIX = 4
PARTS = 2

scale_factor = 0.476986
step_size = 0.25
norm_eps = 1e-06

AXES = ("xh", "z", "c", "y", "xl")
SIZES = (2, 4, 2, 4, 2)
SEQ = ("xh", "z", "c")

NT = (((1,), (1,)), ((), ()))
LOG2E = 1.4426950408889634
PAYLOAD = 80


def shift(x, **moves):
    pairs = []
    for source in range(int(np.prod(SIZES))):
        place = np.unravel_index(source, SIZES)
        target = [(p + moves.get(a, 0)) % n for p, a, n in zip(place, AXES, SIZES)]
        pairs.append((source, int(np.ravel_multi_index(target, SIZES))))
    return lax.ppermute(x, AXES, pairs)


def regroup_kernel(places, n_after, *refs):
    in_refs, out_refs = refs[: len(places)], refs[len(places) + n_after :]
    for in_ref, (out, target) in zip(in_refs, places):
        out_refs[out][target : target + in_ref.shape[0], :] = in_ref[...]


def regroup(groups, after=(), small=(), block=32):
    operands, in_specs, places, shapes = [], [], [], []
    for out, pieces in enumerate(groups):
        target = 0
        for x, start, rows, *columns in pieces:
            column, width = columns or (0, x.shape[1])
            for row in range(start, start + rows, block):
                operands.append(x)
                in_specs.append(
                    pl.BlockSpec((block, width), lambda i, n=row // block, c=column: (n, c))
                )
                places.append((out, target))
                target += block
        shapes.append(jax.ShapeDtypeStruct((target, width), pieces[0][0].dtype))
    return pl.pallas_call(
        functools.partial(regroup_kernel, places, len(after) + len(small)),
        grid=(1,),
        in_specs=in_specs
        + [pl.BlockSpec(memory_space=pltpu.HBM)] * len(after)
        + [pl.BlockSpec(memory_space=pltpu.VMEM)] * len(small),
        out_specs=[pl.BlockSpec(shape.shape, lambda i: (0, 0)) for shape in shapes],
        out_shape=shapes,
        compiler_params=pltpu.CompilerParams(vmem_limit_bytes=20 << 20),
        name="regroup",
    )(*operands, *after, *small)


def project_kernel(q_order, scale, n_after, *refs):
    sources, (own_w_ref, other_w_ref, *refs) = refs[:4], refs[4:]
    q_ref, kv_ref, sent_ref, x_ref, w_ref, sem = refs[n_after:]
    rows = sources[0].shape[0]
    copies = [
        pltpu.make_async_copy(ref, x_ref.at[pl.ds(n * rows, rows), :], sem.at[n])
        for n, ref in enumerate(sources)
    ]
    for copy in copies:
        copy.start()
    for i in range(3):
        for n, weights in enumerate((own_w_ref, other_w_ref)):
            column = (3 * n + i) * HEAD_DIM
            w_ref[:, column : column + HEAD_DIM] = weights[i]
    for first in range(0, 4 * rows, 2 * rows):
        for copy in copies[first // rows : first // rows + 2]:
            copy.wait()
        out = jnp.dot(
            x_ref[first : first + 2 * rows, :], w_ref[...], preferred_element_type=jnp.float32
        )
        own_q = (out[:, :HEAD_DIM] * scale).astype(jnp.bfloat16)
        sent_q = (out[:, 3 * HEAD_DIM : 4 * HEAD_DIM] * scale).astype(jnp.bfloat16)
        for start, count, target in q_order:
            if first <= start < first + 2 * rows:
                piece, target = slice(start - first, start - first + count), slice(target, target + count)
                q_ref[target, :] = own_q[piece]
                sent_ref[target, 2 * HEAD_DIM :] = sent_q[piece]
        piece = slice(first, first + 2 * rows)
        kv_ref[piece, :] = out[:, HEAD_DIM : 3 * HEAD_DIM].astype(jnp.bfloat16)
        sent_ref[piece, : 2 * HEAD_DIM] = out[:, 4 * HEAD_DIM :].astype(jnp.bfloat16)


def project(xs, own_weight, other_weight, q_order, scale, after=()):
    rows, depth = 4 * xs[0].shape[0], own_weight.shape[1]
    widths = [HEAD_DIM, 2 * HEAD_DIM, 3 * HEAD_DIM]
    anywhere, vmem = pl.BlockSpec(memory_space=pltpu.HBM), pl.BlockSpec(memory_space=pltpu.VMEM)
    return pl.pallas_call(
        functools.partial(project_kernel, q_order, scale, len(after)),
        in_specs=[anywhere] * 4 + [vmem] * 2 + [anywhere] * len(after),
        out_specs=[vmem] * 3,
        out_shape=[jax.ShapeDtypeStruct((rows, width), jnp.bfloat16) for width in widths],
        scratch_shapes=[
            pltpu.VMEM((rows, depth), jnp.bfloat16),
            pltpu.VMEM((depth, 6 * HEAD_DIM), jnp.bfloat16),
            pltpu.SemaphoreType.DMA((4,)),
        ],
        compiler_params=pltpu.CompilerParams(vmem_limit_bytes=40 << 20),
        name="project",
    )(*xs, own_weight, other_weight, *after)


def softmax_blocks(q, kv_refs, bk, run_max, acc):
    places = [(ref, i) for ref in kv_refs for i in range(0, ref.shape[0], bk)]
    ones = jnp.ones((bk, HEAD_DIM), jnp.bfloat16)

    def scores_of(n):
        ref, i = places[n]
        return lax.dot_general(
            q, ref[i : i + bk, :HEAD_DIM], NT, preferred_element_type=jnp.float32
        )

    following = scores_of(0)
    for n, (ref, i) in enumerate(places):
        scores = following
        if n + 1 < len(places):
            following = scores_of(n + 1)
        new_max = jnp.max(scores, axis=1, keepdims=True)
        if run_max is not None:
            new_max = jnp.maximum(run_max, new_max)
        probs = jnp.exp2(scores - new_max).astype(jnp.bfloat16)
        values = jnp.concatenate([ref[i : i + bk, HEAD_DIM:], ones], axis=1)
        part = jnp.dot(probs, values, preferred_element_type=jnp.float32)
        acc = part if acc is None else acc * jnp.exp2(run_max - new_max) + part
        run_max = new_max
    return run_max, acc


def attention_kernel(bk, n_q, n_kv, carry_in, n_into, final, *refs):
    if final:
        place_ref, *refs = refs
    q_refs, refs = refs[:n_q], refs[n_q:]
    kv_refs, refs = refs[:n_kv], refs[n_kv:]
    if carry_in:
        acc_in_ref, max_in_ref, *refs = refs
    refs = refs[n_into:]
    if final:
        w_ref, out_ref = refs
    else:
        acc_out_ref, max_out_ref = refs

    q = q_refs[0][...]
    for n in range(1, n_q):
        q = jnp.where(pl.program_id(0) == n, q_refs[n][...], q)
    bq = q.shape[0]
    run_max, acc = None, None
    if carry_in:
        run_max, acc = jnp.max(max_in_ref[...], axis=1, keepdims=True), acc_in_ref[...]
    run_max, acc = softmax_blocks(q, kv_refs, bk, run_max, acc)
    if not final:
        acc_out_ref[...] = acc
        max_out_ref[...] = jnp.broadcast_to(run_max, max_out_ref.shape)
        return

    total = acc[:, HEAD_DIM:]
    attended = (acc[:, :HEAD_DIM] / total).astype(jnp.bfloat16)
    velocity = lax.dot_general(w_ref[...], attended, NT, preferred_element_type=jnp.float32)
    log_sum = run_max + jnp.log2(total)
    high = log_sum.astype(jnp.bfloat16).astype(jnp.float32)
    mid = (log_sum - high).astype(jnp.bfloat16).astype(jnp.float32)
    low = log_sum - high - mid
    lane = lax.broadcasted_iota(jnp.int32, (bq, HEAD_DIM), 1)
    terms = jnp.where(lane == 0, high, jnp.where(lane == 1, mid, low)).astype(jnp.bfloat16)
    row = lax.broadcasted_iota(jnp.int32, (PAYLOAD - 64, HEAD_DIM), 0)
    column = lax.broadcasted_iota(jnp.int32, (PAYLOAD - 64, HEAD_DIM), 1)
    pick = ((row == column) & (row < 3)).astype(jnp.float32).astype(jnp.bfloat16)
    stats = lax.dot_general(pick, terms, NT, preferred_element_type=jnp.float32)
    joined = jnp.concatenate([velocity, stats], axis=0).astype(jnp.bfloat16)
    n_xh, n_z, n_c = out_ref.shape[:3]
    late = pl.program_id(0) % 2
    for core in range(n_c):
        for group, (early_place, late_place) in enumerate(zip(*GROUP_PLACES)):
            t = core * len(GROUP_PLACES[0]) + group
            xh, z = [jnp.where(late == 1, q, p) for p, q in zip(early_place, late_place)]
            out_ref[
                (xh + place_ref[1]) % n_xh, (z + place_ref[2]) % n_z, (core + place_ref[3]) % n_c, 0
            ] = joined[:, t * 128 : (t + 1) * 128]


GROUP_PLACES = (((0, 0), (0, 3), (0, 1), (1, 0)), ((0, 2), (1, 3), (1, 1), (1, 2)))


def attention(qs, kvs, carry=None, fresh=False, blocks=(1, 0), last=None, bk=512):
    bq = qs[0].shape[0]
    stride, offset = blocks
    widths = (2 * HEAD_DIM, HEAD_DIM)
    whole = lambda x: pl.BlockSpec(x.shape, lambda i, *p: (0, 0))
    carried = [
        pl.BlockSpec((bq, width), lambda i, *p: (i * stride + offset, 0)) for width in widths
    ]
    operands = [*qs, *kvs]
    in_specs = [whole(x) for x in operands]
    aliases = {}
    if carry is not None:
        if last is None:
            aliases = {len(operands): 0, len(operands) + 1: 1}
        operands += carry
        in_specs += [pl.BlockSpec(memory_space=pltpu.HBM)] * 2 if fresh else carried
    if last is None:
        prefetch = []
        out_specs = carried
        out_shape = [jax.ShapeDtypeStruct((4 * bq, width), jnp.float32) for width in widths]
    else:
        prefetch = [last[0]]
        operands.append(last[1])
        in_specs.append(whole(last[1]))
        out_specs = pl.BlockSpec(
            (2, 4, 2, 1, PAYLOAD, 128), lambda i, p: (0, 0, 0, (i // 2 + p[0]) % 2, 0, 0)
        )
        out_shape = jax.ShapeDtypeStruct((2, 4, 2, 2, PAYLOAD, 128), jnp.bfloat16)
    read = carry is not None and not fresh
    return pl.pallas_call(
        functools.partial(
            attention_kernel, bk, len(qs), len(kvs), read, len(aliases) if fresh else 0, last is not None
        ),
        grid_spec=pltpu.PrefetchScalarGridSpec(
            num_scalar_prefetch=len(prefetch),
            grid=(len(qs),),
            in_specs=in_specs,
            out_specs=out_specs,
        ),
        out_shape=out_shape,
        input_output_aliases=aliases,
        compiler_params=pltpu.CompilerParams(vmem_limit_bytes=56 << 20),
        name="attention",
    )(*prefetch, *operands)


def combine_kernel(parts_ref, noisy_ref, out_ref):
    velocity = jnp.zeros((64, 128), jnp.float32)
    for head in range(parts_ref.shape[0] // 2):
        logs = []
        for half in range(2):
            terms = parts_ref[2 * head + half, 64:PAYLOAD, :].astype(jnp.float32)
            logs.append(terms[0:1] + terms[1:2] + terms[2:3])
        top = jnp.maximum(logs[0], logs[1])
        first, second = jnp.exp2(logs[0] - top), jnp.exp2(logs[1] - top)
        inverse = 1.0 / (first + second)
        velocity += parts_ref[2 * head, 0:64, :].astype(jnp.float32) * (first * inverse)
        velocity += parts_ref[2 * head + 1, 0:64, :].astype(jnp.float32) * (second * inverse)
    latent = (noisy_ref[...] - step_size * velocity) / scale_factor
    latent = latent.astype(jnp.bfloat16)
    for n in range(out_ref.shape[0]):
        out_ref[n] = latent


def combine(parts, noisy, copies):
    return pl.pallas_call(
        combine_kernel,
        out_shape=jax.ShapeDtypeStruct((copies, 64, 128), jnp.bfloat16),
        name="latent_tile",
    )(parts, noisy)


def placing_matrix():
    side, p, q, i, j = np.meshgrid(*[np.arange(n) for n in (2, 2, 2, 8, 8)], indexing="ij")
    target = (2 * i + p) * 32 + side * 16 + 2 * j + q
    place = np.zeros((512, 512), np.float32)
    place[np.arange(512), target.reshape(-1)] = 1.0
    return place


def decode_kernel(
    ids_ref, own_ref, other_ref, place_ref, first_ref, second_ref, gain_ref, shift_ref, out_ref, wide_ref, half_ref, patch_ref, conv_ref, part_ref, mean_ref, scale_ref, mid_ref
):
    slot, part = pl.program_id(0), pl.program_id(1)
    channels, voxels = conv_ref.shape
    these = pl.ds(pl.multiple_of(part * channels, channels), channels)

    @pl.when((slot == 0) & (part == 0))
    def _():
        for s in range(MAXPIX):
            for half in range(2):
                for side in range(2):
                    n = ids_ref[1 + s * 4 + half * 2 + side]
                    tile = jnp.where(n < 64, own_ref[n % 64], other_ref[n % 64])
                    for pq in range(4):
                        column = (side * 4 + pq) * 64
                        for f in range(2):
                            row = ((s * 2 + f) * 2 + half) * 16
                            wide_ref[row : row + 16, column : column + 64] = tile[
                                pq * 16 : pq * 16 + 16, f * 64 : f * 64 + 64
                            ]
        half_ref[...] = jnp.dot(wide_ref[...], place_ref[...], preferred_element_type=jnp.float32)

    @pl.when(slot >= ids_ref[0])
    def _():
        out_ref[...] = jnp.zeros(out_ref.shape, out_ref.dtype)

    @pl.when((slot < ids_ref[0]) & (part == 0))
    def _():
        halves = half_ref[pl.ds(pl.multiple_of(slot * 64, 64), 64), :]
        region = jnp.concatenate(
            [
                jnp.concatenate([halves[0:16], halves[16:32]], axis=1),
                jnp.concatenate([halves[32:48], halves[48:64]], axis=1),
            ],
            axis=0,
        )
        lane = lax.broadcasted_iota(jnp.int32, region.shape, 1)
        column = lane % 32
        for g in range(3):
            if g == 0:
                across = jnp.where(column == 0, region, pltpu.roll(region, 1, 1))
            elif g == 1:
                across = region
            else:
                across = jnp.where(column == 31, region, pltpu.roll(region, 1023, 1))
            for b in range(3):
                if b == 0:
                    tap = jnp.where(lane < 32, across, pltpu.roll(across, 32, 1))
                elif b == 1:
                    tap = across
                else:
                    tap = jnp.where(lane >= 992, across, pltpu.roll(across, 992, 1))
                row = (b * 3 + g) * 16
                tap = tap.astype(jnp.bfloat16)
                patch_ref[row : row + 16, :] = tap[0:16]
                patch_ref[144 + row : 144 + row + 16, :] = tap[16:32]
    @pl.when(slot < ids_ref[0])
    def _():
        conv_ref[:, :1024] = jnp.dot(
            first_ref[these, :], patch_ref[0:144, :], preferred_element_type=jnp.float32
        )
        conv_ref[:, 1024:] = jnp.dot(
            second_ref[these, :], patch_ref[...], preferred_element_type=jnp.float32
        )
        groups = GROUPS // PARTS
        size = channels // groups
        count = 1.0 / (size * voxels)

        def group_rows(group):
            return slice(group * size, (group + 1) * size)

        def group_means():
            sums = jnp.sum(part_ref[...], axis=1, keepdims=True)
            sums = jnp.sum(sums.reshape(groups, 8, 1), axis=1, keepdims=True) * count
            return jnp.broadcast_to(sums, (groups, size, 128)).reshape(channels, 128)

        for group in range(groups):
            total = jnp.zeros((size, 128), jnp.float32)
            for j in range(0, voxels, 128):
                total += conv_ref[group_rows(group), j : j + 128]
            part_ref[group * 8 : group * 8 + 8, :] = total[:8] + total[8:]
        mean_ref[...] = group_means()
        for group in range(groups):
            mean = mean_ref[group_rows(group), :]
            total = jnp.zeros((size, 128), jnp.float32)
            for j in range(0, voxels, 128):
                apart = conv_ref[group_rows(group), j : j + 128] - mean
                total += apart * apart
            part_ref[group * 8 : group * 8 + 8, :] = total[:8] + total[8:]
        scale_ref[...] = gain_ref[these, :] * (lax.rsqrt(group_means() + norm_eps) * 0.5)
        mid_ref[...] = jnp.broadcast_to(shift_ref[these, :] * 0.5, mid_ref.shape)
        for group in range(groups):
            rows = group_rows(group)
            mean, scale = mean_ref[rows, :], scale_ref[rows, :]
            half_shift = mid_ref[rows, :]
            for j in range(0, voxels, 128):
                half_norm = (conv_ref[rows, j : j + 128] - mean) * scale + half_shift
                out_ref[0, 0, rows, j : j + 128] = (
                    half_norm + half_norm * jnp.tanh(half_norm)
                ).astype(jnp.bfloat16)


def decode(ids, own_tiles, other_tiles, place, first, second, gain, shift_rows):
    channels = first.shape[0]
    whole = lambda shape: pl.BlockSpec(memory_space=pltpu.VMEM)
    rows = channels // PARTS
    return pl.pallas_call(
        decode_kernel,
        grid_spec=pltpu.PrefetchScalarGridSpec(
            num_scalar_prefetch=1,
            grid=(MAXPIX, PARTS),
            in_specs=[
                whole(own_tiles.shape),
                whole(other_tiles.shape),
                whole(place.shape),
                whole(first.shape),
                whole(second.shape),
                whole(gain.shape),
                whole(shift_rows.shape),
            ],
            out_specs=pl.BlockSpec((1, 1, rows, 2048), lambda s, h, ids: (0, s, h, 0)),
            scratch_shapes=[
                pltpu.VMEM((256, 512), jnp.bfloat16),
                pltpu.VMEM((256, 512), jnp.float32),
                pltpu.VMEM((288, 1024), jnp.bfloat16),
                pltpu.VMEM((rows, 2048), jnp.float32),
                pltpu.VMEM((GROUPS // PARTS * 8, 128), jnp.float32),
                pltpu.VMEM((rows, 128), jnp.float32),
                pltpu.VMEM((rows, 128), jnp.float32),
                pltpu.VMEM((rows, 128), jnp.float32),
            ],
        ),
        out_shape=jax.ShapeDtypeStruct((1, MAXPIX, channels, 2048), jnp.bfloat16),
        compiler_params=pltpu.CompilerParams(vmem_limit_bytes=28 << 20),
        name="decode",
    )(ids, own_tiles, other_tiles, place, first, second, gain, shift_rows)


def body(
    tokens,
    project_weight,
    noisy_latent,
    final_weight,
    conv_weight,
    norm_gain,
    norm_shift,
    owner_count,
    intersection,
):
    coordinate = {axis: lax.axis_index(axis).astype(jnp.int32) for axis in AXES}
    head = lax.axis_index(SEQ)

    w = lax.dynamic_slice_in_dim(final_weight, head * HEAD_DIM, HEAD_DIM, axis=0)
    w = w.reshape(HEAD_DIM, LATENT_CH, PATCH).transpose(2, 1, 0).reshape(64, HEAD_DIM)
    noisy = noisy_latent.reshape(-1, LATENT_CH, PATCH).transpose(2, 1, 0).reshape(64, -1)

    rank = lax.axis_index(AXES)
    ends = jnp.cumsum(owner_count, dtype=jnp.int32)
    count = owner_count[rank]
    slots = jnp.minimum(ends[rank] - count + jnp.arange(MAXPIX), intersection.shape[0] - 1)
    wanted = intersection[slots].reshape(-1)
    core = (wanted // 8) % 2
    wanted = (wanted // 16) * 8 + wanted % 8 + 64 * (core != coordinate["c"])
    ids = jnp.concatenate([count[None], wanted]).astype(jnp.int32)

    taps = conv_weight.astype(jnp.float32).reshape(3, -1, conv_weight.shape[1])
    first = (taps[0] + taps[1] + taps[2]).T.astype(jnp.bfloat16)
    second = jnp.concatenate([taps[0] + taps[1], taps[2]], axis=0).T.astype(jnp.bfloat16)
    placing = jnp.asarray(placing_matrix(), jnp.bfloat16)
    decoder = [first, second, norm_gain[:, None], norm_shift[:, None]]

    other_weight = shift(project_weight, c=1)
    below, above, across = shift(tokens, z=1), shift(tokens, z=-1), shift(tokens, xh=1)
    opposite = shift(tokens, xh=1, z=2)
    to_above, to_below, to_across = regroup(
        [
            [(below, 0, 64), (across, 0, 32), (across, 96, 32)],
            [(across, 0, 32), (across, 96, 32), (above, 64, 64)],
            [(below, 32, 64), (above, 32, 64)],
        ],
        small=decoder[:2],
    )
    far_low, far_high, inner = shift(to_above, z=1), shift(to_below, z=-1), shift(to_across, xh=1)

    q_scale = LOG2E * HEAD_DIM**-0.5

    def join(own, received, column, width, after=(), small=()):
        rows = own.shape[0]
        pieces = [(own, 0, rows), (received, 0, rows, column, width)]
        return regroup([pieces], after, small, block=rows)[0]

    early = [tokens, below, above, across]
    early = project(early, project_weight, other_weight, [(0, 256, 0), (256, 256, 256)], q_scale, [to_above])
    received = shift(early[2], c=1)
    kv1 = [join(early[1], received, 0, 2 * HEAD_DIM)]
    kv1 += [shift(kv1[0], y=1), shift(kv1[0], y=3)]
    arrived = [*kv1[1:], far_low, far_high, inner, opposite]
    q1 = join(early[0], received, 2, HEAD_DIM)
    kv1_again = join(early[1], received, 0, 2 * HEAD_DIM, arrived, [ids, w, noisy, *decoder[2:]])
    prepared = [q1, kv1_again]
    kv1.append(shift(kv1_again, y=2))
    q1 = [q1, shift(q1, xl=1)]

    late_order = [(0, 64, 0), (64, 32, 128), (96, 32, 224)]
    late_order += [(128, 32, 256), (160, 32, 352), (192, 64, 64)]
    late_order += [(256, 64, 160), (320, 64, 288), (384, 128, 384)]
    late = [far_low, far_high, inner, opposite]
    q2, own_kv2, sent = project(late, project_weight, other_weight, late_order, q_scale, prepared)
    received = shift(sent, c=1)
    kv2 = [join(own_kv2, received, 0, 2 * HEAD_DIM)]
    kv2 += [shift(kv2[0], y=n) for n in (1, 3, 2)]
    q2 = join(q2, received, 2, HEAD_DIM)
    q2 = [q2, shift(q2, xl=1)]

    carry = attention(q1, [*kv1[:3], kv2[0]], blocks=(2, 0))
    carry = attention(q2, [*kv1[:3], kv2[0]], carry, fresh=True, blocks=(2, 1))
    q_all = [q1[0], q2[0], q1[1], q2[1]]
    place = jnp.stack([coordinate[axis] for axis in ("xl", "xh", "z", "c")])
    parts = attention(q_all, [kv1[3], *kv2[1:]], carry, last=(place, w))
    parts = parts.reshape(-1, PAYLOAD, 128)
    parts = lax.all_to_all(parts, SEQ + ("xl",), split_axis=0, concat_axis=0, tiled=True)
    tile = combine(parts, noisy, 64)

    own_tiles = lax.all_to_all(tile, ("xh", "z", "y", "xl"), split_axis=0, concat_axis=0, tiled=True)
    other_tiles = shift(own_tiles, c=1)
    return decode(ids, own_tiles, other_tiles, placing, *decoder)


def solution(mesh):
    fine = Mesh(mesh.devices.reshape(SIZES), AXES)
    blk = ("y", "xl")
    return jax.shard_map(
        body,
        mesh=fine,
        in_specs=(
            P(SEQ + blk, None),
            P(None, None, SEQ),
            P(SEQ + blk, None),
            P(),
            P(),
            P(),
            P(),
            P(),
            P(),
        ),
        out_specs=P(SEQ + blk, None, None, None),
        check_vma=False,
    )
```

```python
import functools

import jax
import jax.numpy as jnp
import numpy as np
from jax import lax
from jax.experimental import pallas as pl
from jax.experimental.pallas import tpu as pltpu
from jax.sharding import Mesh
from jax.sharding import PartitionSpec as P

HEAD_DIM = 128
LATENT_CH = 16
PATCH = 4
GROUPS = 32
MAXPIX = 4
PARTS = 2

scale_factor = 0.476986
step_size = 0.25
norm_eps = 1e-06

AXES = ("xh", "z", "c", "y", "xl")
SIZES = (2, 4, 2, 4, 2)
SEQ = ("xh", "z", "c")

NT = (((1,), (1,)), ((), ()))
LOG2E = 1.4426950408889634
PAYLOAD = 80


def shift(x, **moves):
    pairs = []
    for source in range(int(np.prod(SIZES))):
        place = np.unravel_index(source, SIZES)
        target = [(p + moves.get(a, 0)) % n for p, a, n in zip(place, AXES, SIZES)]
        pairs.append((source, int(np.ravel_multi_index(target, SIZES))))
    return lax.ppermute(x, AXES, pairs)


def regroup_kernel(places, n_after, *refs):
    in_refs, out_refs = refs[: len(places)], refs[len(places) + n_after :]
    for in_ref, (out, target) in zip(in_refs, places):
        out_refs[out][target : target + in_ref.shape[0], :] = in_ref[...]


def regroup(groups, after=(), small=(), block=32):
    operands, in_specs, places, shapes = [], [], [], []
    for out, pieces in enumerate(groups):
        target = 0
        for x, start, rows, *columns in pieces:
            column, width = columns or (0, x.shape[1])
            for row in range(start, start + rows, block):
                operands.append(x)
                in_specs.append(
                    pl.BlockSpec((block, width), lambda i, n=row // block, c=column: (n, c))
                )
                places.append((out, target))
                target += block
        shapes.append(jax.ShapeDtypeStruct((target, width), pieces[0][0].dtype))
    return pl.pallas_call(
        functools.partial(regroup_kernel, places, len(after) + len(small)),
        grid=(1,),
        in_specs=in_specs
        + [pl.BlockSpec(memory_space=pltpu.HBM)] * len(after)
        + [pl.BlockSpec(memory_space=pltpu.VMEM)] * len(small),
        out_specs=[pl.BlockSpec(shape.shape, lambda i: (0, 0)) for shape in shapes],
        out_shape=shapes,
        compiler_params=pltpu.CompilerParams(vmem_limit_bytes=20 << 20),
        name="regroup",
    )(*operands, *after, *small)


def project_kernel(q_order, scale, n_after, *refs):
    sources, (own_w_ref, other_w_ref, *refs) = refs[:4], refs[4:]
    q_ref, kv_ref, sent_ref, x_ref, w_ref, sem = refs[n_after:]
    rows = sources[0].shape[0]
    copies = [
        pltpu.make_async_copy(ref, x_ref.at[pl.ds(n * rows, rows), :], sem.at[n])
        for n, ref in enumerate(sources)
    ]
    for copy in copies:
        copy.start()
    for i in range(3):
        for n, weights in enumerate((own_w_ref, other_w_ref)):
            column = (3 * n + i) * HEAD_DIM
            w_ref[:, column : column + HEAD_DIM] = weights[i]
    for first in range(0, 4 * rows, 2 * rows):
        for copy in copies[first // rows : first // rows + 2]:
            copy.wait()
        out = jnp.dot(
            x_ref[first : first + 2 * rows, :], w_ref[...], preferred_element_type=jnp.float32
        )
        own_q = (out[:, :HEAD_DIM] * scale).astype(jnp.bfloat16)
        sent_q = (out[:, 3 * HEAD_DIM : 4 * HEAD_DIM] * scale).astype(jnp.bfloat16)
        for start, count, target in q_order:
            if first <= start < first + 2 * rows:
                piece, target = slice(start - first, start - first + count), slice(target, target + count)
                q_ref[target, :] = own_q[piece]
                sent_ref[target, 2 * HEAD_DIM :] = sent_q[piece]
        piece = slice(first, first + 2 * rows)
        kv_ref[piece, :] = out[:, HEAD_DIM : 3 * HEAD_DIM].astype(jnp.bfloat16)
        sent_ref[piece, : 2 * HEAD_DIM] = out[:, 4 * HEAD_DIM :].astype(jnp.bfloat16)


def project(xs, own_weight, other_weight, q_order, scale, after=()):
    rows, depth = 4 * xs[0].shape[0], own_weight.shape[1]
    widths = [HEAD_DIM, 2 * HEAD_DIM, 3 * HEAD_DIM]
    anywhere, vmem = pl.BlockSpec(memory_space=pltpu.HBM), pl.BlockSpec(memory_space=pltpu.VMEM)
    return pl.pallas_call(
        functools.partial(project_kernel, q_order, scale, len(after)),
        in_specs=[anywhere] * 4 + [vmem] * 2 + [anywhere] * len(after),
        out_specs=[vmem] * 3,
        out_shape=[jax.ShapeDtypeStruct((rows, width), jnp.bfloat16) for width in widths],
        scratch_shapes=[
            pltpu.VMEM((rows, depth), jnp.bfloat16),
            pltpu.VMEM((depth, 6 * HEAD_DIM), jnp.bfloat16),
            pltpu.SemaphoreType.DMA((4,)),
        ],
        compiler_params=pltpu.CompilerParams(vmem_limit_bytes=40 << 20),
        name="project",
    )(*xs, own_weight, other_weight, *after)


def softmax_blocks(q, kv_refs, bk, run_max, acc):
    places = [(ref, i) for ref in kv_refs for i in range(0, ref.shape[0], bk)]
    ones = jnp.ones((bk, HEAD_DIM), jnp.bfloat16)

    def scores_of(n):
        ref, i = places[n]
        return lax.dot_general(
            q, ref[i : i + bk, :HEAD_DIM], NT, preferred_element_type=jnp.float32
        )

    following = scores_of(0)
    for n, (ref, i) in enumerate(places):
        scores = following
        if n + 1 < len(places):
            following = scores_of(n + 1)
        new_max = jnp.max(scores, axis=1, keepdims=True)
        if run_max is not None:
            new_max = jnp.maximum(run_max, new_max)
        probs = jnp.exp2(scores - new_max).astype(jnp.bfloat16)
        values = jnp.concatenate([ref[i : i + bk, HEAD_DIM:], ones], axis=1)
        part = jnp.dot(probs, values, preferred_element_type=jnp.float32)
        acc = part if acc is None else acc * jnp.exp2(run_max - new_max) + part
        run_max = new_max
    return run_max, acc


def attention_kernel(bk, n_q, n_kv, carry_in, n_into, final, *refs):
    if final:
        place_ref, *refs = refs
    q_refs, refs = refs[:n_q], refs[n_q:]
    kv_refs, refs = refs[:n_kv], refs[n_kv:]
    if carry_in:
        acc_in_ref, max_in_ref, *refs = refs
    refs = refs[n_into:]
    if final:
        w_ref, out_ref = refs
    else:
        acc_out_ref, max_out_ref = refs

    q = q_refs[0][...]
    for n in range(1, n_q):
        q = jnp.where(pl.program_id(0) == n, q_refs[n][...], q)
    bq = q.shape[0]
    run_max, acc = None, None
    if carry_in:
        run_max, acc = jnp.max(max_in_ref[...], axis=1, keepdims=True), acc_in_ref[...]
    run_max, acc = softmax_blocks(q, kv_refs, bk, run_max, acc)
    if not final:
        acc_out_ref[...] = acc
        max_out_ref[...] = jnp.broadcast_to(run_max, max_out_ref.shape)
        return

    total = acc[:, HEAD_DIM:]
    attended = (acc[:, :HEAD_DIM] / total).astype(jnp.bfloat16)
    velocity = lax.dot_general(w_ref[...], attended, NT, preferred_element_type=jnp.float32)
    log_sum = run_max + jnp.log2(total)
    high = log_sum.astype(jnp.bfloat16).astype(jnp.float32)
    mid = (log_sum - high).astype(jnp.bfloat16).astype(jnp.float32)
    low = log_sum - high - mid
    lane = lax.broadcasted_iota(jnp.int32, (bq, HEAD_DIM), 1)
    terms = jnp.where(lane == 0, high, jnp.where(lane == 1, mid, low)).astype(jnp.bfloat16)
    row = lax.broadcasted_iota(jnp.int32, (PAYLOAD - 64, HEAD_DIM), 0)
    column = lax.broadcasted_iota(jnp.int32, (PAYLOAD - 64, HEAD_DIM), 1)
    pick = ((row == column) & (row < 3)).astype(jnp.float32).astype(jnp.bfloat16)
    stats = lax.dot_general(pick, terms, NT, preferred_element_type=jnp.float32)
    joined = jnp.concatenate([velocity, stats], axis=0).astype(jnp.bfloat16)
    n_xh, n_z, n_c = out_ref.shape[:3]
    late = pl.program_id(0) % 2
    for core in range(n_c):
        for group, (early_place, late_place) in enumerate(zip(*GROUP_PLACES)):
            t = core * len(GROUP_PLACES[0]) + group
            xh, z = [jnp.where(late == 1, q, p) for p, q in zip(early_place, late_place)]
            out_ref[
                (xh + place_ref[1]) % n_xh, (z + place_ref[2]) % n_z, (core + place_ref[3]) % n_c, 0
            ] = joined[:, t * 128 : (t + 1) * 128]


GROUP_PLACES = (((0, 0), (0, 3), (0, 1), (1, 0)), ((0, 2), (1, 3), (1, 1), (1, 2)))


def attention(qs, kvs, carry=None, fresh=False, blocks=(1, 0), last=None, bk=512):
    bq = qs[0].shape[0]
    stride, offset = blocks
    widths = (2 * HEAD_DIM, HEAD_DIM)
    whole = lambda x: pl.BlockSpec(x.shape, lambda i, *p: (0, 0))
    carried = [
        pl.BlockSpec((bq, width), lambda i, *p: (i * stride + offset, 0)) for width in widths
    ]
    operands = [*qs, *kvs]
    in_specs = [whole(x) for x in operands]
    aliases = {}
    if carry is not None:
        if last is None:
            aliases = {len(operands): 0, len(operands) + 1: 1}
        operands += carry
        in_specs += [pl.BlockSpec(memory_space=pltpu.HBM)] * 2 if fresh else carried
    if last is None:
        prefetch = []
        out_specs = carried
        out_shape = [jax.ShapeDtypeStruct((4 * bq, width), jnp.float32) for width in widths]
    else:
        prefetch = [last[0]]
        operands.append(last[1])
        in_specs.append(whole(last[1]))
        out_specs = pl.BlockSpec(
            (2, 4, 2, 1, PAYLOAD, 128), lambda i, p: (0, 0, 0, (i // 2 + p[0]) % 2, 0, 0)
        )
        out_shape = jax.ShapeDtypeStruct((2, 4, 2, 2, PAYLOAD, 128), jnp.bfloat16)
    read = carry is not None and not fresh
    return pl.pallas_call(
        functools.partial(
            attention_kernel, bk, len(qs), len(kvs), read, len(aliases) if fresh else 0, last is not None
        ),
        grid_spec=pltpu.PrefetchScalarGridSpec(
            num_scalar_prefetch=len(prefetch),
            grid=(len(qs),),
            in_specs=in_specs,
            out_specs=out_specs,
        ),
        out_shape=out_shape,
        input_output_aliases=aliases,
        compiler_params=pltpu.CompilerParams(vmem_limit_bytes=36 << 20),
        name="attention",
    )(*prefetch, *operands)


def combine_kernel(parts_ref, noisy_ref, out_ref):
    velocity = jnp.zeros((64, 128), jnp.float32)
    for head in range(parts_ref.shape[0] // 2):
        logs = []
        for half in range(2):
            terms = parts_ref[2 * head + half, 64:PAYLOAD, :].astype(jnp.float32)
            logs.append(terms[0:1] + terms[1:2] + terms[2:3])
        top = jnp.maximum(logs[0], logs[1])
        first, second = jnp.exp2(logs[0] - top), jnp.exp2(logs[1] - top)
        inverse = 1.0 / (first + second)
        velocity += parts_ref[2 * head, 0:64, :].astype(jnp.float32) * (first * inverse)
        velocity += parts_ref[2 * head + 1, 0:64, :].astype(jnp.float32) * (second * inverse)
    latent = (noisy_ref[...] - step_size * velocity) / scale_factor
    latent = latent.astype(jnp.bfloat16)
    for n in range(out_ref.shape[0]):
        out_ref[n] = latent


def combine(parts, noisy, copies):
    return pl.pallas_call(
        combine_kernel,
        out_shape=jax.ShapeDtypeStruct((copies, 64, 128), jnp.bfloat16),
        name="latent_tile",
    )(parts, noisy)


def placing_matrix():
    side, p, q, i, j = np.meshgrid(*[np.arange(n) for n in (2, 2, 2, 8, 8)], indexing="ij")
    target = (2 * i + p) * 32 + side * 16 + 2 * j + q
    place = np.zeros((512, 512), np.float32)
    place[np.arange(512), target.reshape(-1)] = 1.0
    return place


def decode_kernel(
    ids_ref, own_ref, other_ref, place_ref, first_ref, second_ref, gain_ref, shift_ref, out_ref, wide_ref, half_ref, patch_ref, conv_ref, part_ref, mean_ref, scale_ref, mid_ref
):
    slot, part = pl.program_id(0), pl.program_id(1)
    channels, voxels = conv_ref.shape
    these = pl.ds(pl.multiple_of(part * channels, channels), channels)

    @pl.when((slot == 0) & (part == 0))
    def _():
        for s in range(MAXPIX):
            for half in range(2):
                for side in range(2):
                    n = ids_ref[1 + s * 4 + half * 2 + side]
                    tile = jnp.where(n < 64, own_ref[n % 64], other_ref[n % 64])
                    for pq in range(4):
                        column = (side * 4 + pq) * 64
                        for f in range(2):
                            row = ((s * 2 + f) * 2 + half) * 16
                            wide_ref[row : row + 16, column : column + 64] = tile[
                                pq * 16 : pq * 16 + 16, f * 64 : f * 64 + 64
                            ]
        half_ref[...] = jnp.dot(wide_ref[...], place_ref[...], preferred_element_type=jnp.float32)

    @pl.when(slot >= ids_ref[0])
    def _():
        out_ref[...] = jnp.zeros(out_ref.shape, out_ref.dtype)

    @pl.when((slot < ids_ref[0]) & (part == 0))
    def _():
        halves = half_ref[pl.ds(pl.multiple_of(slot * 64, 64), 64), :]
        region = jnp.concatenate(
            [
                jnp.concatenate([halves[0:16], halves[16:32]], axis=1),
                jnp.concatenate([halves[32:48], halves[48:64]], axis=1),
            ],
            axis=0,
        )
        lane = lax.broadcasted_iota(jnp.int32, region.shape, 1)
        column = lane % 32
        for g in range(3):
            if g == 0:
                across = jnp.where(column == 0, region, pltpu.roll(region, 1, 1))
            elif g == 1:
                across = region
            else:
                across = jnp.where(column == 31, region, pltpu.roll(region, 1023, 1))
            for b in range(3):
                if b == 0:
                    tap = jnp.where(lane < 32, across, pltpu.roll(across, 32, 1))
                elif b == 1:
                    tap = across
                else:
                    tap = jnp.where(lane >= 992, across, pltpu.roll(across, 992, 1))
                row = (b * 3 + g) * 16
                tap = tap.astype(jnp.bfloat16)
                patch_ref[row : row + 16, :] = tap[0:16]
                patch_ref[144 + row : 144 + row + 16, :] = tap[16:32]
    @pl.when(slot < ids_ref[0])
    def _():
        conv_ref[:, :1024] = jnp.dot(
            first_ref[these, :], patch_ref[0:144, :], preferred_element_type=jnp.float32
        )
        conv_ref[:, 1024:] = jnp.dot(
            second_ref[these, :], patch_ref[...], preferred_element_type=jnp.float32
        )
        groups = GROUPS // PARTS
        size = channels // groups
        count = 1.0 / (size * voxels)

        def group_rows(group):
            return slice(group * size, (group + 1) * size)

        def group_means():
            sums = jnp.sum(part_ref[...], axis=1, keepdims=True)
            sums = jnp.sum(sums.reshape(groups, 8, 1), axis=1, keepdims=True) * count
            return jnp.broadcast_to(sums, (groups, size, 128)).reshape(channels, 128)

        for group in range(groups):
            total = jnp.zeros((size, 128), jnp.float32)
            for j in range(0, voxels, 128):
                total += conv_ref[group_rows(group), j : j + 128]
            part_ref[group * 8 : group * 8 + 8, :] = total[:8] + total[8:]
        mean_ref[...] = group_means()
        for group in range(groups):
            mean = mean_ref[group_rows(group), :]
            total = jnp.zeros((size, 128), jnp.float32)
            for j in range(0, voxels, 128):
                apart = conv_ref[group_rows(group), j : j + 128] - mean
                total += apart * apart
            part_ref[group * 8 : group * 8 + 8, :] = total[:8] + total[8:]
        scale_ref[...] = gain_ref[these, :] * (lax.rsqrt(group_means() + norm_eps) * 0.5)
        mid_ref[...] = jnp.broadcast_to(shift_ref[these, :] * 0.5, mid_ref.shape)
        for group in range(groups):
            rows = group_rows(group)
            mean, scale = mean_ref[rows, :], scale_ref[rows, :]
            half_shift = mid_ref[rows, :]
            for j in range(0, voxels, 128):
                half_norm = (conv_ref[rows, j : j + 128] - mean) * scale + half_shift
                out_ref[0, 0, rows, j : j + 128] = (
                    half_norm + half_norm * jnp.tanh(half_norm)
                ).astype(jnp.bfloat16)


def decode(ids, own_tiles, other_tiles, place, first, second, gain, shift_rows):
    channels = first.shape[0]
    whole = lambda shape: pl.BlockSpec(memory_space=pltpu.VMEM)
    rows = channels // PARTS
    return pl.pallas_call(
        decode_kernel,
        grid_spec=pltpu.PrefetchScalarGridSpec(
            num_scalar_prefetch=1,
            grid=(MAXPIX, PARTS),
            in_specs=[
                whole(own_tiles.shape),
                whole(other_tiles.shape),
                whole(place.shape),
                whole(first.shape),
                whole(second.shape),
                whole(gain.shape),
                whole(shift_rows.shape),
            ],
            out_specs=pl.BlockSpec((1, 1, rows, 2048), lambda s, h, ids: (0, s, h, 0)),
            scratch_shapes=[
                pltpu.VMEM((256, 512), jnp.bfloat16),
                pltpu.VMEM((256, 512), jnp.float32),
                pltpu.VMEM((288, 1024), jnp.bfloat16),
                pltpu.VMEM((rows, 2048), jnp.float32),
                pltpu.VMEM((GROUPS // PARTS * 8, 128), jnp.float32),
                pltpu.VMEM((rows, 128), jnp.float32),
                pltpu.VMEM((rows, 128), jnp.float32),
                pltpu.VMEM((rows, 128), jnp.float32),
            ],
        ),
        out_shape=jax.ShapeDtypeStruct((1, MAXPIX, channels, 2048), jnp.bfloat16),
        compiler_params=pltpu.CompilerParams(vmem_limit_bytes=28 << 20),
        name="decode",
    )(ids, own_tiles, other_tiles, place, first, second, gain, shift_rows)


def body(
    tokens,
    project_weight,
    noisy_latent,
    final_weight,
    conv_weight,
    norm_gain,
    norm_shift,
    owner_count,
    intersection,
):
    coordinate = {axis: lax.axis_index(axis).astype(jnp.int32) for axis in AXES}
    head = lax.axis_index(SEQ)

    w = lax.dynamic_slice_in_dim(final_weight, head * HEAD_DIM, HEAD_DIM, axis=0)
    w = w.reshape(HEAD_DIM, LATENT_CH, PATCH).transpose(2, 1, 0).reshape(64, HEAD_DIM)
    noisy = noisy_latent.reshape(-1, LATENT_CH, PATCH).transpose(2, 1, 0).reshape(64, -1)

    rank = lax.axis_index(AXES)
    ends = jnp.cumsum(owner_count, dtype=jnp.int32)
    count = owner_count[rank]
    slots = jnp.minimum(ends[rank] - count + jnp.arange(MAXPIX), intersection.shape[0] - 1)
    wanted = intersection[slots].reshape(-1)
    core = (wanted // 8) % 2
    wanted = (wanted // 16) * 8 + wanted % 8 + 64 * (core != coordinate["c"])
    ids = jnp.concatenate([count[None], wanted]).astype(jnp.int32)

    taps = conv_weight.astype(jnp.float32).reshape(3, -1, conv_weight.shape[1])
    first = (taps[0] + taps[1] + taps[2]).T.astype(jnp.bfloat16)
    second = jnp.concatenate([taps[0] + taps[1], taps[2]], axis=0).T.astype(jnp.bfloat16)
    placing = jnp.asarray(placing_matrix(), jnp.bfloat16)
    decoder = [first, second, norm_gain[:, None], norm_shift[:, None]]

    other_weight = shift(project_weight, c=1)
    below, above, across = shift(tokens, z=1), shift(tokens, z=-1), shift(tokens, xh=1)
    opposite = shift(tokens, xh=1, z=2)
    to_above, to_below, to_across = regroup(
        [
            [(below, 0, 64), (across, 0, 32), (across, 96, 32)],
            [(across, 0, 32), (across, 96, 32), (above, 64, 64)],
            [(below, 32, 64), (above, 32, 64)],
        ],
        small=decoder[:2],
    )
    far_low, far_high, inner = shift(to_above, z=1), shift(to_below, z=-1), shift(to_across, xh=1)

    q_scale = LOG2E * HEAD_DIM**-0.5

    def join(own, received, column, width, after=(), small=()):
        rows = own.shape[0]
        pieces = [(own, 0, rows), (received, 0, rows, column, width)]
        return regroup([pieces], after, small, block=rows)[0]

    early = [tokens, below, above, across]
    early = project(early, project_weight, other_weight, [(0, 256, 0), (256, 256, 256)], q_scale, [to_above])
    received = shift(early[2], c=1)
    kv1 = [join(early[1], received, 0, 2 * HEAD_DIM)]
    kv1 += [shift(kv1[0], y=1), shift(kv1[0], y=3)]
    arrived = [*kv1[1:], far_low, far_high, inner, opposite]
    q1 = join(early[0], received, 2, HEAD_DIM)
    kv1_again = join(early[1], received, 0, 2 * HEAD_DIM, arrived, [ids, w, noisy, *decoder[2:]])
    prepared = [q1, kv1_again]
    kv1.append(shift(kv1_again, y=2))
    q1 = [q1, shift(q1, xl=1)]

    late_order = [(0, 64, 0), (64, 32, 128), (96, 32, 224)]
    late_order += [(128, 32, 256), (160, 32, 352), (192, 64, 64)]
    late_order += [(256, 64, 160), (320, 64, 288), (384, 128, 384)]
    late = [far_low, far_high, inner, opposite]
    q2, own_kv2, sent = project(late, project_weight, other_weight, late_order, q_scale, prepared)
    received = shift(sent, c=1)
    kv2 = [join(own_kv2, received, 0, 2 * HEAD_DIM)]
    kv2 += [shift(kv2[0], y=n) for n in (1, 3, 2)]
    q2 = join(q2, received, 2, HEAD_DIM)
    q2 = [q2, shift(q2, xl=1)]

    carry = attention(q1, [*kv1[:3], kv2[0]], blocks=(2, 0))
    carry = attention(q2, [*kv1[:3], kv2[0]], carry, fresh=True, blocks=(2, 1))
    q_all = [q1[0], q2[0], q1[1], q2[1]]
    place = jnp.stack([coordinate[axis] for axis in ("xl", "xh", "z", "c")])
    carry = attention(q_all, [kv1[3]], carry)
    parts = attention(q_all, kv2[1:], carry, last=(place, w))
    parts = parts.reshape(-1, PAYLOAD, 128)
    parts = lax.all_to_all(parts, SEQ + ("xl",), split_axis=0, concat_axis=0, tiled=True)
    tile = combine(parts, noisy, 64)

    own_tiles = lax.all_to_all(tile, ("xh", "z", "y", "xl"), split_axis=0, concat_axis=0, tiled=True)
    other_tiles = shift(own_tiles, c=1)
    return decode(ids, own_tiles, other_tiles, placing, *decoder)


def solution(mesh):
    fine = Mesh(mesh.devices.reshape(SIZES), AXES)
    blk = ("y", "xl")
    return jax.shard_map(
        body,
        mesh=fine,
        in_specs=(
            P(SEQ + blk, None),
            P(None, None, SEQ),
            P(SEQ + blk, None),
            P(),
            P(),
            P(),
            P(),
            P(),
            P(),
        ),
        out_specs=P(SEQ + blk, None, None, None),
        check_vma=False,
    )
```
